32 devices in a mesh: song: 2 (over x), tm: 8 (over z, y), freq: 2 (over core).
Axes of the slice: x: 2, y: 2, z: 4, core: 2. Of those that a mesh axis runs over, the one named last changes fastest.
Arguments:
- latent: bfloat16 [256, 128, 1024], P(None, 'freq', ('song', 'tm')), parts along dimension 2, as said below
- mel_noisy: float32 [128, 1024], P('freq', ('song', 'tm')), parts along dimension 1, may hold values from -6 to 6
- time_shift: float32 [512], P('song'), parts along dimension 0, may hold values from -3 to 3
- first_gain: float32 [256], replicated, may hold values from 0.5 to 1.5
- first_shift: float32 [256], replicated, may hold values from -3 to 3
- conv_first: bfloat16 [3, 3, 256, 256], replicated, may hold values from -0.125 to 0.125
- second_gain: float32 [256], replicated, may hold values from 0.5 to 1.5
- second_shift: float32 [256], replicated, may hold values from -3 to 3
- conv_second: bfloat16 [3, 3, 256, 256], replicated, may hold values from -0.125 to 0.125
- second_bias: float32 [256], replicated, may hold values from -3 to 3
- out_proj: float32 [256], replicated, may hold values from -0.375 to 0.375
- pre_weight: bfloat16 [1536, 7, 128], P('tm'), may hold values from -0.1875 to 0.1875
- pre_bias: float32 [1536], replicated, may hold values from -3 to 3
- up_weight: bfloat16 [1536, 8, 768], P(None, None, 'freq'), may hold values from -0.109375 to 0.109375
- up_bias: float32 [768], P('freq'), may hold values from -3 to 3
Outputs:
- mel_next: float32 [128, 1024], P('freq', ('song', 'tm')), parts along dimension 1
- vocal: bfloat16 [768, 4096], P('freq', ('song', 'tm')), parts along dimension 1
The draws below stay inside these ranges and needn't reach their ends.
There are 2 independent parts, one for each index of `song`. The reference program is written for one: setup_inputs(seed, part) draws one part's arguments, and reference() takes and returns one part's arrays. A program takes and returns all parts, laid end to end along the dimension named above; an argument that names none is the same for every part. Nothing has to cross between parts.
Inputs may be any that keep to these rules, and one draw needn't show every extreme that they name: `latent`: activations of the block's input, of order one to some tens.
All inputs are finite; a program needn't handle non-finite values.
Results may differ from the reference program's by a relative error of at most 0.0055.
Values may be sent and summed in bfloat16 or wider, within the bound.
A program may use at most 192 MiB of HBM per device.

```python
import jax
import jax.numpy as jnp
from jax import lax

CHANNELS = 256
MELS = 128
GROUPS = 32
PRE_WIDTH = 1536
UP_WIDTH = 768
FRAMES = 512


def draw_latent(key, part):
    key_base, key_chan, key_frame = jax.random.split(key, 3)
    base = jnp.clip(jax.random.normal(key_base, (CHANNELS, MELS, FRAMES), jnp.float32), -5.0, 5.0)
    ramp = 3.0 ** (jnp.arange(FRAMES, dtype=jnp.float32) / FRAMES - 0.5)
    chan_scale = 10.0 ** (jax.random.uniform(key_chan, (CHANNELS,), jnp.float32) - 0.5)
    rough = jax.random.uniform(key_frame, (FRAMES,), jnp.float32, 0.5, 2.0)
    values = base * chan_scale[:, None, None] * (rough * ramp)[None, None, :]
    return values.astype(jnp.bfloat16)


def steps_of(key, dims, pieces, least, top_value):
    level, own = 1.0, jax.random.fold_in(key, 6)
    for position, shards_of in pieces:
        heights = jnp.exp(jax.random.uniform(jax.random.fold_in(own, position), (shards_of,), jnp.float32, least / len(pieces), top_value / len(pieces)))
        level = level * jnp.repeat(heights, dims[position] // shards_of).reshape([-1 if axis == position else 1 for axis in range(len(dims))])
    return level


def normal_values(rng, shape, spread, reach, pieces=(), kind=jnp.bfloat16):
    array = jax.random.normal(rng, shape, jnp.float32) * spread
    if len(pieces) > 0:
        array = steps_of(rng, shape, pieces, -0.22, 0.18) * array
    return jnp.clip(array, min=-reach, max=reach).astype(kind)


def setup_inputs(seed: int = 0, part: int = 0) -> dict:
    key_of = jax.random.split(jax.random.key(seed), 16)
    part_splits = jax.random.split(jax.random.fold_in(key_of[15], part), 16)
    return {
        "latent": draw_latent(jax.random.fold_in(jax.random.fold_in(key_of[15], part), 71), part),
        "mel_noisy": normal_values(part_splits[1], (MELS, FRAMES), 1.0, 6.0, ((0, 2), (1, 8)), jnp.float32),
        "time_shift": normal_values(part_splits[2], (CHANNELS,), 0.5, 3.0, (), jnp.float32),
        "first_gain": jnp.clip(jax.random.uniform(key_of[3], (CHANNELS,), jnp.float32, 0.5, 1.5), 0.5, 1.5),
        "first_shift": normal_values(key_of[4], (CHANNELS,), 0.5, 3.0, (), jnp.float32),
        "conv_first": normal_values(key_of[5], (3, 3, CHANNELS, CHANNELS), (9 * CHANNELS) ** -0.5, 0.125),
        "second_gain": jnp.clip(jax.random.uniform(key_of[6], (CHANNELS,), jnp.float32, 0.5, 1.5), 0.5, 1.5),
        "second_shift": normal_values(key_of[7], (CHANNELS,), 0.5, 3.0, (), jnp.float32),
        "conv_second": normal_values(key_of[8], (3, 3, CHANNELS, CHANNELS), (9 * CHANNELS) ** -0.5, 0.125),
        "second_bias": normal_values(key_of[9], (CHANNELS,), 0.5, 3.0, (), jnp.float32),
        "out_proj": normal_values(key_of[10], (CHANNELS,), CHANNELS ** -0.5, 0.375, (), jnp.float32),
        "pre_weight": normal_values(key_of[11], (PRE_WIDTH, 7, MELS), (7 * MELS) ** -0.5, 0.1875, ((0, 8),)),
        "pre_bias": normal_values(key_of[12], (PRE_WIDTH,), 0.5, 3.0, (), jnp.float32),
        "up_weight": normal_values(key_of[13], (PRE_WIDTH, 8, UP_WIDTH), (2 * PRE_WIDTH) ** -0.5, 0.109375, ((2, 2),)),
        "up_bias": normal_values(key_of[14], (UP_WIDTH,), 0.5, 3.0, ((0, 2),), jnp.float32),
    }


EPSILON = 1e-05
STEP_SIZE = 0.25

def norm_silu(values_in, gain, shift):
    chans, bins, frames = values_in.shape
    values = values_in.astype(jnp.float32).reshape(GROUPS, chans // GROUPS, bins, frames)
    count = float(chans // GROUPS * bins * frames)
    mean = lax.optimization_barrier(jnp.sum(values, axis=(1, 2, 3))) / count
    var = lax.optimization_barrier(jnp.sum(values * values, axis=(1, 2, 3))) / count - mean * mean
    scaled = (values - mean[:, None, None, None]) * lax.rsqrt(var + EPSILON)[:, None, None, None]
    scaled = scaled.reshape(chans, bins, frames) * gain[:, None, None] + shift[:, None, None]
    return jax.nn.silu(scaled).astype(jnp.bfloat16)

def conv_three(active, weight):
    bins, frames = (active.shape[1], active.shape[2])
    padded = jnp.pad(active.astype(jnp.float32), ((0, 0), (1, 1), (1, 1)))
    wide = weight.astype(jnp.float32)
    total = jnp.zeros((weight.shape[3], bins, frames), jnp.float32)
    for i in range(3):
        for j in range(3):
            total = total + jnp.einsum('io,ift->oft', wide[i, j], padded[:, i:i + bins, j:j + frames])
    return total

def up_tap(up_weight, k, feats):
    return jnp.dot(up_weight[:, k, :].T, feats, preferred_element_type=jnp.float32)

def reference(latent, mel_noisy, time_shift, first_gain, first_shift, conv_first, second_gain, second_shift, conv_second, second_bias, out_proj, pre_weight, pre_bias, up_weight, up_bias):
    active = norm_silu(latent, first_gain, first_shift)
    first_out = (conv_three(active, conv_first) + time_shift[:, None, None]).astype(jnp.bfloat16)
    second_in = norm_silu(first_out, second_gain, second_shift)
    hidden = latent.astype(jnp.float32) + conv_three(second_in, conv_second) + second_bias[:, None, None]
    velocity = lax.optimization_barrier(jnp.sum(out_proj[:, None, None] * hidden, axis=0))
    mel_next = mel_noisy + STEP_SIZE * velocity
    mel_in = mel_next.astype(jnp.bfloat16)
    frames = mel_in.shape[1]
    padded = jnp.pad(mel_in, ((0, 0), (3, 3)))
    total = jnp.zeros((pre_weight.shape[0], frames), jnp.float32)
    for k in range(7):
        total = total + jnp.dot(pre_weight[:, k, :], padded[:, k:k + frames], preferred_element_type=jnp.float32)
    features = (total + pre_bias[:, None]).astype(jnp.bfloat16)
    framed = jnp.pad(features, ((0, 0), (1, 1)))
    middle = framed[:, 1:frames + 1]
    before = framed[:, 0:frames]
    after = framed[:, 2:frames + 2]
    phases = []
    for p in range(4):
        term = up_tap(up_weight, p + 2, middle)
        if p <= 1:
            term = term + up_tap(up_weight, p + 6, before)
        else:
            term = term + up_tap(up_weight, p - 2, after)
        phases.append(term)
    stacked = jnp.stack(phases, axis=2).reshape(up_weight.shape[2], 4 * frames)
    vocal = (stacked + up_bias[:, None]).astype(jnp.bfloat16)
    return (mel_next, vocal)
```

```python
import functools

import jax
import jax.numpy as jnp
from jax import lax
from jax.experimental import pallas as pl
from jax.experimental.pallas import tpu as pltpu
from jax.sharding import PartitionSpec as P

GROUPS = 32
EPSILON = 1e-05
STEP_SIZE = 0.25
MESH = pl.DeviceIdType.MESH
F32 = jnp.float32
BF16 = jnp.bfloat16
NT = (((1,), (1,)), ((), ()))


def dot(a, b):
    return jnp.dot(a, b, preferred_element_type=F32)


def dot_nt(a, b):
    return lax.dot_general(a, b, NT, preferred_element_type=F32)


def three_parts(x):
    hi = x.astype(BF16)
    rest = x - hi.astype(F32)
    mid = rest.astype(BF16)
    low = (rest - mid.astype(F32)).astype(BF16)
    return hi, mid, low


def block_kernel(
    n_tm, n_f,
    lat, mel, tshift, gain1, shift1, w1, gain2, shift2, w2, bias2, proj,
    mel_out, mt_out,
    stats1, stats2, stage_l, stage_r, halo_l, halo_r, halo_b, corner_l, corner_r,
    act_l, act_r, spread, first, gpad, zt, z_part, z_before, z_after, turned,
    s1_send, s1_recv, s2_send, s2_recv, h_send, h_recv, z_send, z_recv,
):
    bins, frames, chans = lat.shape
    n = n_tm * n_f
    tm = lax.axis_index("tm")
    f = lax.axis_index("freq")
    me = tm * n_f + f
    other = 1 - f
    has_left = tm > 0
    has_right = tm < n_tm - 1

    def peer_of(k):
        p = lax.rem(me + k, n)
        return p, {"tm": p // n_f, "freq": lax.rem(p, n_f)}

    barrier = pltpu.get_barrier_semaphore()

    def greet(k, c):
        pl.semaphore_signal(barrier, inc=1, device_id=peer_of(k)[1], device_id_type=MESH)
        return c

    lax.fori_loop(1, n, greet, 0)

    sub8 = lax.broadcasted_iota(jnp.int32, (bins, 8, chans), 1)
    head = lat[:, 0:16, :].astype(F32)[:, 0:8, :]
    tail = lat[:, frames - 16 : frames, :].astype(F32)[:, 8:16, :]
    stage_l[...] = jnp.sum(jnp.where(sub8 == 0, head, 0.0), axis=1).astype(BF16)
    stage_r[...] = jnp.sum(jnp.where(sub8 == 7, tail, 0.0), axis=1).astype(BF16)

    pl.semaphore_wait(barrier, n - 1)

    def remote(src, dst, send, recv, to):
        return pltpu.make_async_remote_copy(
            src_ref=src, dst_ref=dst, send_sem=send, recv_sem=recv, device_id=to, device_id_type=MESH
        )

    edge = pl.multiple_of((1 - f) * (bins - 16), 16)
    to_left = [{"tm": tm - 1, "freq": f}, {"tm": tm - 1, "freq": other}]
    to_right = [{"tm": tm + 1, "freq": f}, {"tm": tm + 1, "freq": other}]
    partner = {"tm": tm, "freq": other}
    h_bin = remote(lat.at[(1 - f) * (bins - 1)], halo_b, h_send.at[0], h_recv.at[0], partner)
    h_bin.start()
    go_left = [
        remote(stage_l, halo_r, h_send.at[1], h_recv.at[1], to_left[0]),
        remote(stage_l.at[pl.ds(edge, 16)], corner_r, h_send.at[2], h_recv.at[2], to_left[1]),
    ]
    go_right = [
        remote(stage_r, halo_l, h_send.at[3], h_recv.at[3], to_right[0]),
        remote(stage_r.at[pl.ds(edge, 16)], corner_l, h_send.at[4], h_recv.at[4], to_right[1]),
    ]

    @pl.when(has_left)
    def _():
        for c in go_left:
            c.start()

    @pl.when(has_right)
    def _():
        for c in go_right:
            c.start()

    def fold(x):
        return jnp.sum(x.reshape(-1, 8, chans), axis=0)

    def stat_step(b, carry):
        s, q = carry
        x = lat[pl.ds(b * 4, 4)].astype(F32)
        return s + fold(x), q + fold(x * x)

    zero8 = jnp.zeros((8, chans), F32)
    s, q = lax.fori_loop(0, bins // 4, stat_step, (zero8, zero8))

    def send_stats(s, q, stats, send, recv):
        stats[me] = jnp.concatenate(
            [jnp.sum(s, axis=0, keepdims=True), jnp.sum(q, axis=0, keepdims=True)], axis=1
        )

        def go(k, c):
            _, to = peer_of(k)
            remote(stats.at[me], stats.at[me], send.at[k], recv.at[me], to).start()
            return c

        lax.fori_loop(1, n, go, 0)

    def take_stats(stats, send, recv):
        def wait(k, c):
            p, to = peer_of(k)
            remote(stats.at[me], stats.at[p], send.at[k], recv.at[p], to).wait_recv()
            return c

        lax.fori_loop(1, n, wait, 0)
        total = jnp.sum(stats[...], axis=0)
        both = jnp.concatenate(
            [
                jnp.broadcast_to(total[:, :chans], (8, chans)),
                jnp.broadcast_to(total[:, chans:], (8, chans)),
            ],
            axis=0,
        )
        size = chans // GROUPS
        gi = lax.broadcasted_iota(jnp.int32, (chans, chans), 0) // size
        gj = lax.broadcasted_iota(jnp.int32, (chans, chans), 1) // size
        same = (gi == gj).astype(F32)
        sums = jnp.dot(both, same, preferred_element_type=F32, precision=lax.Precision.HIGHEST)
        count = float(size * bins * frames * n)
        mean = sums[0:1] / count
        var = sums[8:9] / count - mean * mean
        return mean, lax.rsqrt(var + EPSILON)

    def end_stats(stats, send, recv):
        def wait(k, c):
            p, to = peer_of(k)
            remote(stats.at[me], stats.at[me], send.at[k], recv.at[me], to).wait_send()
            return c

        lax.fori_loop(1, n, wait, 0)

    send_stats(s, q, stats1, s1_send, s1_recv)

    p_row = proj[...]
    hi, mid, low = [x.astype(F32) for x in three_parts(p_row)]
    row = lax.broadcasted_iota(jnp.int32, (16, chans), 0)
    parts = jnp.where(row == 0, hi, jnp.where(row == 1, mid, jnp.where(row == 2, low, 0.0))).astype(BF16)
    row24 = lax.broadcasted_iota(jnp.int32, (32, chans), 0)
    taps = jnp.zeros((32, chans), F32)
    for i in range(3):
        for j in range(3):
            wv = jnp.sum(dot_nt(parts, w2[3 * i + j]), axis=0, keepdims=True)
            a, b, _ = three_parts(wv)
            taps = jnp.where(row24 == 8 * j + i, a.astype(F32), taps)
            taps = jnp.where(row24 == 8 * j + 3 + i, b.astype(F32), taps)
    taps = taps.astype(BF16)
    direct = jnp.where(row24 == 9, hi, jnp.where(row24 == 12, mid, jnp.where(row24 == 14, low, 0.0))).astype(BF16)
    const = jnp.sum(p_row * bias2[...], axis=1, keepdims=True)

    h_bin.wait()

    @pl.when(has_left)
    def _():
        for c in go_left:
            c.wait_send()
        for c in go_right:
            c.wait_recv()

    @pl.when(has_right)
    def _():
        for c in go_right:
            c.wait_send()
        for c in go_left:
            c.wait_recv()

    mean, inv = take_stats(stats1, s1_send, s1_recv)
    scale = inv * gain1[...]
    shift = shift1[...]

    def silu(x, mean, scale, shift):
        y = (x - mean) * scale + shift
        h = 0.5 * y
        return h + h * jnp.tanh(h)

    left_on = jnp.where(has_left, 1.0, 0.0).astype(F32)
    right_on = jnp.where(has_right, 1.0, 0.0).astype(F32)

    def edge_act(ref, present):
        x = ref[...].astype(F32)
        return jnp.where(present, silu(x, mean, scale, shift), 0.0)

    act_l[...] = edge_act(halo_l, has_left)
    act_r[...] = edge_act(halo_r, has_right)
    cl = edge_act(corner_l, has_left)
    cr = edge_act(corner_r, has_right)
    pick = f * 15
    r16 = lax.broadcasted_iota(jnp.int32, (16, chans), 0)
    cl = jnp.sum(jnp.where(r16 == pick, cl, 0.0), axis=0, keepdims=True)
    cr = jnp.sum(jnp.where(r16 == pick, cr, 0.0), axis=0, keepdims=True)
    rows = lax.broadcasted_iota(jnp.int32, (frames, chans), 0)

    def put(at, x, left, right):
        spread[at, :, 0:chans] = jnp.where(rows == 0, left, pltpu.roll(x, 1, 0)).astype(BF16)
        spread[at, :, chans : 2 * chans] = x.astype(BF16)
        spread[at, :, 2 * chans : 3 * chans] = jnp.where(
            rows == frames - 1, right, pltpu.roll(x, frames - 1, 0)
        ).astype(BF16)

    put((1 - f) * (bins + 1), silu(halo_b[...].astype(F32), mean, scale, shift), cl, cr)
    spread[f * (bins + 1)] = jnp.zeros(spread.shape[1:], BF16)

    def norm_step(b, c):
        for u in range(4):
            at = b * 4 + u
            x = silu(lat[at].astype(F32), mean, scale, shift)
            put(at + 1, x, act_l[pl.ds(at, 1), :], act_r[pl.ds(at, 1), :])
        return c

    lax.fori_loop(0, bins // 4, norm_step, 0)

    nb = 8
    moved = tshift[...]

    def conv_step(b, carry):
        s, q = carry
        acc = jnp.zeros((nb * frames, chans), F32)
        for i in range(3):
            part = spread[pl.ds(b * nb + i, nb)].reshape(nb * frames, 3 * chans)
            acc = acc + dot(part, w1[i])
        out = (acc + moved).astype(BF16)
        first[pl.ds(b * nb, nb)] = out.reshape(nb, frames, chans)
        x = out.astype(F32)
        return s + fold(x), q + fold(x * x)

    s, q = lax.fori_loop(0, bins // nb, conv_step, (zero8, zero8))
    end_stats(stats1, s1_send, s1_recv)
    send_stats(s, q, stats2, s2_send, s2_recv)

    gpad[...] = jnp.zeros(gpad.shape, F32)
    mean2, inv2 = take_stats(stats2, s2_send, s2_recv)
    scale2 = inv2 * gain2[...]
    low2 = shift2[...]
    vb = 4
    sub = lax.broadcasted_iota(jnp.int32, (8, frames), 0)

    def tap_step(b, c):
        x = first[pl.ds(b * vb, vb)].reshape(vb * frames, chans).astype(F32)
        act = silu(x, mean2, scale2, low2).astype(BF16)
        raw = lat[pl.ds(b * vb, vb)].reshape(vb * frames, chans)
        g = dot_nt(taps, act) + dot_nt(direct, raw)
        for u in range(vb):
            at = b * vb + u
            own = mel[pl.ds(at, 1), :] * (1.0 / STEP_SIZE) + const
            for j in range(3):
                piece = g[8 * j : 8 * j + 8, u * frames : (u + 1) * frames]
                if j == 1:
                    piece = jnp.where(sub == 7, own, piece)
                gpad[j, at + 2, :, 0:frames] = piece
        return c

    lax.fori_loop(0, bins // vb, tap_step, 0)
    end_stats(stats2, s2_send, s2_recv)

    tall = bins + 8
    subs = lax.broadcasted_iota(jnp.int32, (tall, 8, 128), 1)
    total = jnp.zeros((tall, 128), F32)
    for j in range(3):
        comb = jnp.zeros((tall, 8, 128), F32)
        for i in range(3):
            mine = (subs == i) | (subs == i + 3)
            if i == 1:
                mine = mine | (subs >= 6)
            comb = jnp.where(mine, gpad[j, i : i + tall], comb)
        rowsum = jnp.sum(comb, axis=1)
        total = total + (pltpu.roll(rowsum, 2 - j, 1) if j < 2 else rowsum)
    z = jnp.concatenate([total * STEP_SIZE, jnp.zeros((128 - tall, 128), F32)], axis=0)
    wide = frames + 8
    zt[...] = jnp.transpose(z)[0:wide]

    top = frames - 8
    z_own = remote(zt, z_part, z_send.at[0], z_recv.at[0], partner)
    z_left = [
        remote(zt.at[pl.ds(0, 8)], z_after.at[0], z_send.at[1], z_recv.at[1], to_left[0]),
        remote(zt.at[pl.ds(0, 8)], z_after.at[1], z_send.at[2], z_recv.at[2], to_left[1]),
    ]
    z_right = [
        remote(zt.at[pl.ds(top, 16)], z_before.at[0], z_send.at[3], z_recv.at[3], to_right[0]),
        remote(zt.at[pl.ds(top, 16)], z_before.at[1], z_send.at[4], z_recv.at[4], to_right[1]),
    ]

    @pl.when(has_left)
    def _():
        for c in z_left:
            c.start()

    @pl.when(has_right)
    def _():
        for c in z_right:
            c.start()

    z_own.start()

    @pl.when(has_left)
    def _():
        for c in z_left:
            c.wait_send()
        for c in z_right:
            c.wait_recv()

    @pl.when(has_right)
    def _():
        for c in z_right:
            c.wait_send()
        for c in z_left:
            c.wait_recv()

    z_own.wait()

    def lane_place(mine, theirs):
        shape = mine.shape
        lane = lax.broadcasted_iota(jnp.int32, shape, 1)
        low = jnp.where(f == 0, mine, theirs)
        high = jnp.where(f == 0, theirs, mine)
        low = jnp.where(lane <= bins, pltpu.roll(low, 127, 1), 0.0)
        high = jnp.where(lane >= bins - 1, pltpu.roll(high, bins - 1, 1), 0.0)
        return low + high

    span = frames + 16
    center = lane_place(zt[...], z_part[...])
    before = jnp.where(has_left, lane_place(z_before[0], z_before[1]), 0.0)
    after = jnp.where(has_right, lane_place(z_after[0], z_after[1]), 0.0)
    big = jnp.concatenate([center, jnp.zeros((8, 128), F32)], axis=0)
    big = pltpu.roll(big, 7, 0)
    r_b = lax.broadcasted_iota(jnp.int32, (16, 128), 0)
    before = jnp.where(r_b >= 1, before, 0.0)
    before = jnp.concatenate([before, jnp.zeros((span - 16, 128), F32)], axis=0)
    before = pltpu.roll(before, span - 1, 0)
    after = jnp.concatenate([after, jnp.zeros((span - 8, 128), F32)], axis=0)
    after = pltpu.roll(after, frames + 7, 0)
    pos = lax.broadcasted_iota(jnp.int32, (span, 128), 0) - 8 + tm * frames
    whole = jnp.where((pos >= 0) & (pos < n_tm * frames), big + before + after, 0.0)
    mt_out[...] = whole.astype(BF16)
    turned[...] = jnp.transpose(
        jnp.concatenate([whole[8 : 8 + frames], jnp.zeros((128 - frames, 128), F32)], axis=0)
    )
    mel_out[...] = turned[pl.ds(pl.multiple_of(f * bins, 8), bins), 0:frames]


def up_kernel(
    n_tm, frames,
    mt, pre, pre_bias, up, up_bias, out, taps_in, spread, acc,
):
    step = pl.program_id(0)
    span, bins = mt.shape
    n_taps, block, _ = pre.shape
    kernel_taps = up.shape[0] // block
    tm = lax.axis_index("tm")

    @pl.when(step == 0)
    def _():
        m = mt[...].astype(F32)
        for k in range(n_taps):
            s = (n_taps // 2 - k) % span
            taps_in[:, k * bins : (k + 1) * bins] = (pltpu.roll(m, s, 0) if s else m).astype(BF16)
        r = lax.broadcasted_iota(jnp.int32, spread.shape, 0)
        c = lax.broadcasted_iota(jnp.int32, spread.shape, 1)
        spread[...] = (c // kernel_taps == r).astype(F32).astype(BF16)
        acc[...] = jnp.zeros(acc.shape, F32)

    total = jnp.zeros((span, block), F32)
    for k in range(n_taps):
        total = total + dot_nt(taps_in[:, k * bins : (k + 1) * bins], pre[k])
    pos = lax.broadcasted_iota(jnp.int32, (span, block), 0) - 8 + tm * frames
    feats = jnp.where((pos >= 0) & (pos < n_tm * frames), total + pre_bias[...], 0.0).astype(BF16)
    wide = dot(feats, spread[...])
    lane = lax.broadcasted_iota(jnp.int32, wide.shape, 1)
    tap = lax.rem(lane, kernel_taps)
    wide = jnp.where(tap < 4, wide, pltpu.roll(wide, 1, 0))
    phase = lax.rem(lane[0:frames], 4)
    pieces = []
    for p in range(4):
        start = 8 + (1 if p >= 2 else 0)
        pieces.append(jnp.where(phase == (p + 2) % 4, wide[start : start + frames], 0.0).astype(BF16))
    acc[...] += dot(jnp.concatenate(pieces, axis=0), up[...])

    @pl.when(step == pl.num_programs(0) - 1)
    def _():
        rows = acc.shape[0]
        done = (acc[...] + up_bias[...]).astype(BF16).astype(F32)
        r = lax.broadcasted_iota(jnp.int32, (rows, rows), 0)
        c = lax.broadcasted_iota(jnp.int32, (rows, rows), 1)
        perm = (r == lax.rem(c, 4) * frames + c // 4).astype(F32).astype(BF16)
        out[...] = dot(jnp.transpose(done).astype(BF16), perm).astype(BF16)


def shards(
    latent, mel_noisy, time_shift, first_gain, first_shift, conv_first, second_gain,
    second_shift, conv_second, second_bias, out_proj, pre_weight, pre_bias, up_weight, up_bias,
):
    chans, bins, frames = latent.shape
    n_tm, n_f = lax.axis_size("tm"), lax.axis_size("freq")
    n = n_tm * n_f
    lat = jnp.transpose(latent, (1, 2, 0))
    pre_full = lax.all_gather(jnp.transpose(pre_weight, (1, 0, 2)), "tm", axis=1, tiled=True)
    vec = lambda v: v.reshape(1, -1)
    vmem = pl.BlockSpec(memory_space=pltpu.VMEM)
    span = frames + 16
    dma = pltpu.SemaphoreType.DMA
    mel_next, mt = pl.pallas_call(
        functools.partial(block_kernel, n_tm, n_f),
        out_shape=(
            jax.ShapeDtypeStruct((bins, frames), F32),
            jax.ShapeDtypeStruct((span, 128), BF16),
        ),
        in_specs=[vmem] * 11,
        out_specs=(vmem, vmem),
        scratch_shapes=[
            pltpu.VMEM((n, 1, 2 * chans), F32),
            pltpu.VMEM((n, 1, 2 * chans), F32),
            pltpu.VMEM((bins, chans), BF16),
            pltpu.VMEM((bins, chans), BF16),
            pltpu.VMEM((bins, chans), BF16),
            pltpu.VMEM((bins, chans), BF16),
            pltpu.VMEM((frames, chans), BF16),
            pltpu.VMEM((16, chans), BF16),
            pltpu.VMEM((16, chans), BF16),
            pltpu.VMEM((bins, chans), F32),
            pltpu.VMEM((bins, chans), F32),
            pltpu.VMEM((bins + 2, frames, 3 * chans), BF16),
            pltpu.VMEM((bins, frames, chans), BF16),
            pltpu.VMEM((3, bins + 16, 8, 128), F32),
            pltpu.VMEM((frames + 8, 128), F32),
            pltpu.VMEM((frames + 8, 128), F32),
            pltpu.VMEM((2, 16, 128), F32),
            pltpu.VMEM((2, 8, 128), F32),
            pltpu.VMEM((128, 128), F32),
            dma((n,)), dma((n,)), dma((n,)), dma((n,)),
            dma((5,)), dma((5,)), dma((5,)), dma((5,)),
        ],
        compiler_params=pltpu.CompilerParams(
            collective_id=0, has_side_effects=True, vmem_limit_bytes=40 * 2**20
        ),
        cost_estimate=pl.CostEstimate(
            flops=2 * 9 * bins * frames * chans * chans, bytes_accessed=5 * 2**20, transcendentals=0
        ),
    )(
        lat, mel_noisy, vec(time_shift), vec(first_gain), vec(first_shift),
        conv_first.reshape(3, 3 * chans, chans), vec(second_gain), vec(second_shift),
        conv_second.reshape(9, chans, chans), vec(second_bias), vec(out_proj),
    )

    n_taps, width, mels = pre_full.shape
    k_taps, outs = up_weight.shape[1], up_weight.shape[2]
    block = 256
    vocal = pl.pallas_call(
        functools.partial(up_kernel, n_tm, frames),
        grid=(width // block,),
        out_shape=jax.ShapeDtypeStruct((outs, 4 * frames), BF16),
        in_specs=[
            pl.BlockSpec((span, mels), lambda i: (0, 0)),
            pl.BlockSpec((n_taps, block, mels), lambda i: (0, i, 0)),
            pl.BlockSpec((1, block), lambda i: (0, i)),
            pl.BlockSpec((block * k_taps, outs), lambda i: (i, 0)),
            pl.BlockSpec((1, outs), lambda i: (0, 0)),
        ],
        out_specs=pl.BlockSpec((outs, 4 * frames), lambda i: (0, 0)),
        scratch_shapes=[
            pltpu.VMEM((span, n_taps * mels), BF16),
            pltpu.VMEM((block, block * k_taps), BF16),
            pltpu.VMEM((4 * frames, outs), F32),
        ],
        compiler_params=pltpu.CompilerParams(vmem_limit_bytes=40 * 2**20),
        cost_estimate=pl.CostEstimate(
            flops=2 * 4 * frames * width * k_taps * outs, bytes_accessed=13 * 2**20, transcendentals=0
        ),
    )(mt, pre_full, vec(pre_bias), up_weight.reshape(width * k_taps, outs), vec(up_bias))
    return (mel_next, vocal)


def solution(mesh):
    in_specs = (
        P(None, "freq", ("song", "tm")),
        P("freq", ("song", "tm")),
        P("song"),
        P(),
        P(),
        P(),
        P(),
        P(),
        P(),
        P(),
        P(),
        P("tm", None, None),
        P(),
        P(None, None, "freq"),
        P("freq"),
    )
    out_specs = (P("freq", ("song", "tm")), P("freq", ("song", "tm")))
    return jax.shard_map(shards, mesh=mesh, in_specs=in_specs, out_specs=out_specs, check_vma=False)
```

```python
import functools

import jax
import jax.numpy as jnp
from jax import lax
from jax.experimental import pallas as pl
from jax.experimental.pallas import tpu as pltpu
from jax.sharding import PartitionSpec as P

GROUPS = 32
EPSILON = 1e-05
STEP_SIZE = 0.25
MESH = pl.DeviceIdType.MESH
F32 = jnp.float32
BF16 = jnp.bfloat16
NT = (((1,), (1,)), ((), ()))


def dot(a, b):
    return jnp.dot(a, b, preferred_element_type=F32)


def dot_nt(a, b):
    return lax.dot_general(a, b, NT, preferred_element_type=F32)


def three_parts(x):
    hi = x.astype(BF16)
    rest = x - hi.astype(F32)
    mid = rest.astype(BF16)
    low = (rest - mid.astype(F32)).astype(BF16)
    return hi, mid, low


def block_kernel(
    n_tm, n_f, fused,
    lat_h, mel_h, tshift_h, gain1_h, shift1_h, w1_h, gain2_h, shift2_h, w2_h, bias2_h, proj_h,
    pre_h, pre_bias_h, up_h, up_bias_h,
    mel_out, vocal,
    lat, mel, tshift, gain1, shift1, w1, gain2, shift2, w2, bias2, proj, pre_bias, up_bias,
    pre, up,
    stats1, stats2, stage_l, stage_r, halo_l, halo_r, halo_b, corner_l, corner_r,
    act_l, act_r, spread, first, gpad, zt, z_part, z_before, z_after, turned,
    taps_in, repeat, feats, wide_f, acc,
    in_sem, up_sem, own_sem,
    s1_send, s1_recv, s2_send, s2_recv, h_send, h_recv, z_send, z_recv,
    p_send, p_recv, fw_send, ft_send, ft_recv,
):
    bins, frames, chans = lat.shape
    n = n_tm * n_f
    tm = lax.axis_index("tm")
    f = lax.axis_index("freq")
    me = tm * n_f + f
    other = 1 - f
    has_left = tm > 0
    has_right = tm < n_tm - 1

    def peer_of(k):
        p = lax.rem(me + k, n)
        return p, {"tm": p // n_f, "freq": lax.rem(p, n_f)}

    barrier = pltpu.get_barrier_semaphore()
    loads = [
        pltpu.make_async_copy(src, dst, in_sem.at[i])
        for i, (src, dst) in enumerate([
            (lat_h, lat), (w2_h, w2), (w1_h, w1), (mel_h, mel), (tshift_h, tshift), (gain1_h, gain1),
            (shift1_h, shift1), (gain2_h, gain2), (shift2_h, shift2), (bias2_h, bias2), (proj_h, proj),
            (pre_bias_h, pre_bias), (up_bias_h, up_bias),
        ])
    ]

    def greet(k, c):
        pl.semaphore_signal(barrier, inc=1, device_id=peer_of(k)[1], device_id_type=MESH)
        return c

    lax.fori_loop(1, n, greet, 0)
    for c in loads:
        c.start()
    loads[0].wait()
    load_up = pltpu.make_async_copy(up_h, up, up_sem)
    load_up.start()

    sub8 = lax.broadcasted_iota(jnp.int32, (bins, 8, chans), 1)
    head = lat[:, 0:16, :].astype(F32)[:, 0:8, :]
    tail = lat[:, frames - 16 : frames, :].astype(F32)[:, 8:16, :]
    stage_l[...] = jnp.sum(jnp.where(sub8 == 0, head, 0.0), axis=1).astype(BF16)
    stage_r[...] = jnp.sum(jnp.where(sub8 == 7, tail, 0.0), axis=1).astype(BF16)

    pl.semaphore_wait(barrier, n - 1)

    def remote(src, dst, send, recv, to):
        return pltpu.make_async_remote_copy(
            src_ref=src, dst_ref=dst, send_sem=send, recv_sem=recv, device_id=to, device_id_type=MESH
        )

    edge = pl.multiple_of((1 - f) * (bins - 16), 16)
    to_left = [{"tm": tm - 1, "freq": f}, {"tm": tm - 1, "freq": other}]
    to_right = [{"tm": tm + 1, "freq": f}, {"tm": tm + 1, "freq": other}]
    partner = {"tm": tm, "freq": other}
    h_bin = remote(lat.at[(1 - f) * (bins - 1)], halo_b, h_send.at[0], h_recv.at[0], partner)
    h_bin.start()
    go_left = [
        remote(stage_l, halo_r, h_send.at[1], h_recv.at[1], to_left[0]),
        remote(stage_l.at[pl.ds(edge, 16)], corner_r, h_send.at[2], h_recv.at[2], to_left[1]),
    ]
    go_right = [
        remote(stage_r, halo_l, h_send.at[3], h_recv.at[3], to_right[0]),
        remote(stage_r.at[pl.ds(edge, 16)], corner_l, h_send.at[4], h_recv.at[4], to_right[1]),
    ]

    @pl.when(has_left)
    def _():
        for c in go_left:
            c.start()

    @pl.when(has_right)
    def _():
        for c in go_right:
            c.start()

    def fold(x):
        return jnp.sum(x.reshape(-1, 8, chans), axis=0)

    def stat_step(b, carry):
        s, q = carry
        x = lat[pl.ds(b * 4, 4)].astype(F32)
        return s + fold(x), q + fold(x * x)

    zero8 = jnp.zeros((8, chans), F32)
    s, q = lax.fori_loop(0, bins // 4, stat_step, (zero8, zero8))

    def send_stats(s, q, stats, send, recv):
        stats[me] = jnp.concatenate(
            [jnp.sum(s, axis=0, keepdims=True), jnp.sum(q, axis=0, keepdims=True)], axis=1
        )

        def go(k, c):
            _, to = peer_of(k)
            remote(stats.at[me], stats.at[me], send.at[k], recv.at[me], to).start()
            return c

        lax.fori_loop(1, n, go, 0)

    def take_stats(stats, send, recv):
        def wait(k, c):
            p, to = peer_of(k)
            remote(stats.at[me], stats.at[p], send.at[k], recv.at[p], to).wait_recv()
            return c

        lax.fori_loop(1, n, wait, 0)
        total = jnp.sum(stats[...], axis=0)
        both = jnp.concatenate(
            [
                jnp.broadcast_to(total[:, :chans], (8, chans)),
                jnp.broadcast_to(total[:, chans:], (8, chans)),
            ],
            axis=0,
        )
        size = chans // GROUPS
        gi = lax.broadcasted_iota(jnp.int32, (chans, chans), 0) // size
        gj = lax.broadcasted_iota(jnp.int32, (chans, chans), 1) // size
        same = (gi == gj).astype(F32)
        sums = jnp.dot(both, same, preferred_element_type=F32, precision=lax.Precision.HIGHEST)
        count = float(size * bins * frames * n)
        mean = sums[0:1] / count
        var = sums[8:9] / count - mean * mean
        return mean, lax.rsqrt(var + EPSILON)

    def end_stats(stats, send, recv):
        def wait(k, c):
            p, to = peer_of(k)
            remote(stats.at[me], stats.at[me], send.at[k], recv.at[me], to).wait_send()
            return c

        lax.fori_loop(1, n, wait, 0)

    send_stats(s, q, stats1, s1_send, s1_recv)

    half_n = n_tm // n_f
    slot = lax.rem(tm, half_n)
    beside = tm + 1 - 2 * lax.rem(tm, 2)
    holder = f == tm // half_n

    def push(k):
        to = jnp.where(k == 0, beside, lax.rem(tm + 2 * k, n_tm))
        return remote(pre_h, pre.at[:, slot], p_send.at[k], p_recv.at[slot], {"tm": to, "freq": f})

    def forward(j):
        d = 2 * j + lax.rem(tm, 2)
        return d, remote(pre.at[:, d], pre.at[:, d], fw_send.at[j], p_recv.at[d], {"tm": beside, "freq": f})

    if fused:
        own_pre = pltpu.make_async_copy(pre_h, pre.at[:, slot], own_sem)
    else:
        own_pre = pltpu.make_async_copy(pre_h, pre, own_sem)
        own_pre.start()

    def gather_start():
        @pl.when(holder)
        def _():
            own_pre.start()

            def go(k, c):
                push(k).start()
                return c

            lax.fori_loop(0, n_tm // 2, go, 0)

    def gather_forward():
        def go(j, c):
            d, copy = forward(j)

            @pl.when(d + f * half_n != tm)
            def _():
                copy.wait_recv()
                copy.start()

            return c

        lax.fori_loop(0, half_n // 2, go, 0)

    def gather_end():
        @pl.when(holder)
        def _():
            own_pre.wait()

            def wait(k, c):
                push(k).wait_send()
                return c

            lax.fori_loop(0, n_tm // 2, wait, 0)

        def rest(j, c):
            d, copy = forward(j)

            @pl.when(d + f * half_n != tm)
            def _():
                copy.wait_send()

            e = 2 * j + 1 - lax.rem(tm, 2)
            remote(pre.at[:, e], pre.at[:, e], fw_send.at[j], p_recv.at[e], {"tm": beside, "freq": f}).wait_recv()
            return c

        lax.fori_loop(0, half_n // 2, rest, 0)

    if fused:
        gather_start()

    for c in loads[1:]:
        c.wait()

    k_taps = repeat.shape[1] // 128
    r = lax.broadcasted_iota(jnp.int32, repeat.shape, 0)
    c = lax.broadcasted_iota(jnp.int32, repeat.shape, 1)
    repeat[...] = (c // k_taps == r).astype(F32).astype(BF16)
    acc[...] = jnp.zeros(acc.shape, F32)
    gpad[...] = jnp.zeros(gpad.shape, F32)

    p_row = proj[...]
    hi, mid, low = [x.astype(F32) for x in three_parts(p_row)]
    row = lax.broadcasted_iota(jnp.int32, (16, chans), 0)
    parts = jnp.where(row == 0, hi, jnp.where(row == 1, mid, jnp.where(row == 2, low, 0.0))).astype(BF16)
    row24 = lax.broadcasted_iota(jnp.int32, (32, chans), 0)
    taps = jnp.zeros((32, chans), F32)
    for i in range(3):
        for j in range(3):
            wv = jnp.sum(dot_nt(parts, w2[3 * i + j]), axis=0, keepdims=True)
            a, b, _ = three_parts(wv)
            taps = jnp.where(row24 == 8 * j + i, a.astype(F32), taps)
            taps = jnp.where(row24 == 8 * j + 3 + i, b.astype(F32), taps)
    taps = taps.astype(BF16)
    direct = jnp.where(row24 == 9, hi, jnp.where(row24 == 12, mid, jnp.where(row24 == 14, low, 0.0))).astype(BF16)
    const = jnp.sum(p_row * bias2[...], axis=1, keepdims=True)

    h_bin.wait()

    @pl.when(has_left)
    def _():
        for c in go_left:
            c.wait_send()
        for c in go_right:
            c.wait_recv()

    @pl.when(has_right)
    def _():
        for c in go_right:
            c.wait_send()
        for c in go_left:
            c.wait_recv()

    mean, inv = take_stats(stats1, s1_send, s1_recv)
    scale = inv * gain1[...]
    shift = shift1[...]

    def silu(x, mean, scale, shift):
        y = (x - mean) * scale + shift
        h = 0.5 * y
        return h + h * jnp.tanh(h)

    left_on = jnp.where(has_left, 1.0, 0.0).astype(F32)
    right_on = jnp.where(has_right, 1.0, 0.0).astype(F32)

    def edge_act(ref, present):
        x = ref[...].astype(F32)
        return jnp.where(present, silu(x, mean, scale, shift), 0.0)

    act_l[...] = edge_act(halo_l, has_left)
    act_r[...] = edge_act(halo_r, has_right)
    cl = edge_act(corner_l, has_left)
    cr = edge_act(corner_r, has_right)
    pick = f * 15
    r16 = lax.broadcasted_iota(jnp.int32, (16, chans), 0)
    cl = jnp.sum(jnp.where(r16 == pick, cl, 0.0), axis=0, keepdims=True)
    cr = jnp.sum(jnp.where(r16 == pick, cr, 0.0), axis=0, keepdims=True)
    rows = lax.broadcasted_iota(jnp.int32, (frames, chans), 0)

    def put(at, x, left, right):
        spread[at, :, 0:chans] = jnp.where(rows == 0, left, pltpu.roll(x, 1, 0)).astype(BF16)
        spread[at, :, chans : 2 * chans] = x.astype(BF16)
        spread[at, :, 2 * chans : 3 * chans] = jnp.where(
            rows == frames - 1, right, pltpu.roll(x, frames - 1, 0)
        ).astype(BF16)

    put((1 - f) * (bins + 1), silu(halo_b[...].astype(F32), mean, scale, shift), cl, cr)
    spread[f * (bins + 1)] = jnp.zeros(spread.shape[1:], BF16)

    def norm_step(b, c):
        for u in range(4):
            at = b * 4 + u
            x = silu(lat[at].astype(F32), mean, scale, shift)
            put(at + 1, x, act_l[pl.ds(at, 1), :], act_r[pl.ds(at, 1), :])
        return c

    lax.fori_loop(0, bins // 4, norm_step, 0)

    nb = 8
    moved = tshift[...]

    def conv_step(b, carry):
        s, q = carry
        acc = jnp.zeros((nb * frames, chans), F32)
        for i in range(3):
            part = spread[pl.ds(b * nb + i, nb)].reshape(nb * frames, 3 * chans)
            acc = acc + dot(part, w1[i])
        out = (acc + moved).astype(BF16)
        first[pl.ds(b * nb, nb)] = out.reshape(nb, frames, chans)
        x = out.astype(F32)
        return s + fold(x), q + fold(x * x)

    s, q = lax.fori_loop(0, bins // nb, conv_step, (zero8, zero8))
    end_stats(stats1, s1_send, s1_recv)
    send_stats(s, q, stats2, s2_send, s2_recv)

    if fused:
        gather_forward()
    mean2, inv2 = take_stats(stats2, s2_send, s2_recv)
    scale2 = inv2 * gain2[...]
    low2 = shift2[...]
    vb = 4
    sub = lax.broadcasted_iota(jnp.int32, (8, frames), 0)

    def tap_step(b, c):
        x = first[pl.ds(b * vb, vb)].reshape(vb * frames, chans).astype(F32)
        act = silu(x, mean2, scale2, low2).astype(BF16)
        raw = lat[pl.ds(b * vb, vb)].reshape(vb * frames, chans)
        g = dot_nt(taps, act) + dot_nt(direct, raw)
        for u in range(vb):
            at = b * vb + u
            own = mel[pl.ds(at, 1), :] * (1.0 / STEP_SIZE) + const
            for j in range(3):
                piece = g[8 * j : 8 * j + 8, u * frames : (u + 1) * frames]
                if j == 1:
                    piece = jnp.where(sub == 7, own, piece)
                gpad[j, at + 2, :, 0:frames] = piece
        return c

    lax.fori_loop(0, bins // vb, tap_step, 0)
    end_stats(stats2, s2_send, s2_recv)

    tall = bins + 8
    subs = lax.broadcasted_iota(jnp.int32, (tall, 8, 128), 1)
    total = jnp.zeros((tall, 128), F32)
    for j in range(3):
        comb = jnp.zeros((tall, 8, 128), F32)
        for i in range(3):
            mine = (subs == i) | (subs == i + 3)
            if i == 1:
                mine = mine | (subs >= 6)
            comb = jnp.where(mine, gpad[j, i : i + tall], comb)
        rowsum = jnp.sum(comb, axis=1)
        total = total + (pltpu.roll(rowsum, 2 - j, 1) if j < 2 else rowsum)
    z = jnp.concatenate([total * STEP_SIZE, jnp.zeros((128 - tall, 128), F32)], axis=0)
    wide = frames + 8
    zt[...] = jnp.transpose(z)[0:wide]

    top = frames - 8
    z_own = remote(zt, z_part, z_send.at[0], z_recv.at[0], partner)
    z_left = [
        remote(zt.at[pl.ds(0, 8)], z_after.at[0], z_send.at[1], z_recv.at[1], to_left[0]),
        remote(zt.at[pl.ds(0, 8)], z_after.at[1], z_send.at[2], z_recv.at[2], to_left[1]),
    ]
    z_right = [
        remote(zt.at[pl.ds(top, 16)], z_before.at[0], z_send.at[3], z_recv.at[3], to_right[0]),
        remote(zt.at[pl.ds(top, 16)], z_before.at[1], z_send.at[4], z_recv.at[4], to_right[1]),
    ]

    @pl.when(has_left)
    def _():
        for c in z_left:
            c.start()

    @pl.when(has_right)
    def _():
        for c in z_right:
            c.start()

    z_own.start()

    @pl.when(has_left)
    def _():
        for c in z_left:
            c.wait_send()
        for c in z_right:
            c.wait_recv()

    @pl.when(has_right)
    def _():
        for c in z_right:
            c.wait_send()
        for c in z_left:
            c.wait_recv()

    z_own.wait()

    def lane_place(mine, theirs):
        shape = mine.shape
        lane = lax.broadcasted_iota(jnp.int32, shape, 1)
        low = jnp.where(f == 0, mine, theirs)
        high = jnp.where(f == 0, theirs, mine)
        low = jnp.where(lane <= bins, pltpu.roll(low, 127, 1), 0.0)
        high = jnp.where(lane >= bins - 1, pltpu.roll(high, bins - 1, 1), 0.0)
        return low + high

    span = frames + 16
    center = lane_place(zt[...], z_part[...])
    before = jnp.where(has_left, lane_place(z_before[0], z_before[1]), 0.0)
    after = jnp.where(has_right, lane_place(z_after[0], z_after[1]), 0.0)
    big = jnp.concatenate([center, jnp.zeros((8, 128), F32)], axis=0)
    big = pltpu.roll(big, 7, 0)
    r_b = lax.broadcasted_iota(jnp.int32, (16, 128), 0)
    before = jnp.where(r_b >= 1, before, 0.0)
    before = jnp.concatenate([before, jnp.zeros((span - 16, 128), F32)], axis=0)
    before = pltpu.roll(before, span - 1, 0)
    after = jnp.concatenate([after, jnp.zeros((span - 8, 128), F32)], axis=0)
    after = pltpu.roll(after, frames + 7, 0)
    pos = lax.broadcasted_iota(jnp.int32, (span, 128), 0) - 8 + tm * frames
    whole = jnp.where((pos >= 0) & (pos < n_tm * frames), big + before + after, 0.0)
    turned[...] = jnp.transpose(
        jnp.concatenate([whole[8 : 8 + frames], jnp.zeros((128 - frames, 128), F32)], axis=0)
    )
    mel_out[...] = turned[pl.ds(pl.multiple_of(f * bins, 8), bins), 0:frames]

    m = whole.astype(BF16).astype(F32)
    n_taps, mels = pre.shape[0], pre.shape[-1]
    width = feats.shape[2]
    for k in range(n_taps):
        s = (n_taps // 2 - k) % span
        taps_in[:, k * mels : (k + 1) * mels] = (pltpu.roll(m, s, 0) if s else m).astype(BF16)
    if fused:
        gather_end()
    else:
        own_pre.wait()
    made = jnp.zeros((span, width), F32)
    for k in range(n_taps):
        made = made + dot_nt(taps_in[:, k * mels : (k + 1) * mels], pre[k].reshape(width, mels))
    pos = lax.broadcasted_iota(jnp.int32, (span, width), 0) - 8 + tm * frames
    made = made + pre_bias[:, pl.ds(pl.multiple_of(f * width, 128), width)]
    feats[f] = jnp.where((pos >= 0) & (pos < n_tm * frames), made, 0.0).astype(BF16)
    swap = remote(feats.at[f], feats.at[f], ft_send, ft_recv, partner)
    swap.start()
    load_up.wait()

    group = wide_f.shape[1] // k_taps
    rep = 128 * k_taps
    lane = lax.broadcasted_iota(jnp.int32, (span, rep), 1)
    upper = lax.rem(lane, k_taps) < 4
    phase = lax.rem(lane[0:frames], 4)

    def upsample(h):
        for g in range(width // group):
            for t in range(group // 128):
                at = g * group + t * 128
                wide = dot(feats[h, :, at : at + 128], repeat[...])
                wide = jnp.where(upper, wide, pltpu.roll(wide, 1, 0))
                for p in range(4):
                    start = 8 + (1 if p >= 2 else 0)
                    wide_f[p * frames : (p + 1) * frames, t * rep : (t + 1) * rep] = jnp.where(
                        phase == (p + 2) % 4, wide[start : start + frames], 0.0
                    ).astype(BF16)
            row = pl.multiple_of((h * width + g * group) * k_taps, 128)
            acc[...] += dot(wide_f[...], up[pl.ds(row, group * k_taps), :])

    upsample(f)
    swap.wait()
    upsample(other)
    done = (acc[...] + up_bias[...]).astype(BF16).astype(F32)
    r = lax.broadcasted_iota(jnp.int32, (4 * frames, 4 * frames), 0)
    c = lax.broadcasted_iota(jnp.int32, (4 * frames, 4 * frames), 1)
    perm = (r == lax.rem(c, 4) * frames + c // 4).astype(F32).astype(BF16)
    vocal[...] = dot(jnp.transpose(done).astype(BF16), perm).astype(BF16)


def shards(
    latent, mel_noisy, time_shift, first_gain, first_shift, conv_first, second_gain,
    second_shift, conv_second, second_bias, out_proj, pre_weight, pre_bias, up_weight, up_bias,
):
    chans, bins, frames = latent.shape
    n_tm, n_f = lax.axis_size("tm"), lax.axis_size("freq")
    n = n_tm * n_f
    lat = jnp.transpose(latent, (1, 2, 0))
    vec = lambda v: v.reshape(1, -1)
    vmem = pl.BlockSpec(memory_space=pltpu.VMEM)
    hbm = pl.BlockSpec(memory_space=pl.ANY)
    span = frames + 16
    dma = pltpu.SemaphoreType.DMA
    pre = jnp.transpose(pre_weight, (1, 0, 2))
    n_taps, rows, mels = pre.shape
    k_taps, outs = up_weight.shape[1], up_weight.shape[2]
    half = n_tm * rows // n_f
    fused = rows % 16 == 0 and n_tm % 4 == 0
    if fused:
        held = (n_taps, n_tm // n_f, rows, mels)
    else:
        held = (n_taps, half, mels)
        pre = lax.all_gather(pre, "tm", axis=1, tiled=True)
        pre = lax.dynamic_slice_in_dim(pre, lax.axis_index("freq") * half, half, axis=1)
    operands = (
        lat, mel_noisy, vec(time_shift), vec(first_gain), vec(first_shift),
        conv_first.reshape(3, 3 * chans, chans), vec(second_gain), vec(second_shift),
        conv_second.reshape(9, chans, chans), vec(second_bias), vec(out_proj),
        pre, vec(pre_bias), up_weight.reshape(-1, outs), vec(up_bias),
    )
    copies = [pltpu.VMEM(x.shape, x.dtype) for x in operands[:11] + (operands[12], operands[14])]
    return pl.pallas_call(
        functools.partial(block_kernel, n_tm, n_f, fused),
        out_shape=(
            jax.ShapeDtypeStruct((bins, frames), F32),
            jax.ShapeDtypeStruct((outs, 4 * frames), BF16),
        ),
        in_specs=[hbm] * 15,
        out_specs=(vmem, vmem),
        scratch_shapes=copies + [
            pltpu.VMEM(held, BF16),
            pltpu.VMEM(operands[13].shape, BF16),
            pltpu.VMEM((n, 1, 2 * chans), F32),
            pltpu.VMEM((n, 1, 2 * chans), F32),
            pltpu.VMEM((bins, chans), BF16),
            pltpu.VMEM((bins, chans), BF16),
            pltpu.VMEM((bins, chans), BF16),
            pltpu.VMEM((bins, chans), BF16),
            pltpu.VMEM((frames, chans), BF16),
            pltpu.VMEM((16, chans), BF16),
            pltpu.VMEM((16, chans), BF16),
            pltpu.VMEM((bins, chans), F32),
            pltpu.VMEM((bins, chans), F32),
            pltpu.VMEM((bins + 2, frames, 3 * chans), BF16),
            pltpu.VMEM((bins, frames, chans), BF16),
            pltpu.VMEM((3, bins + 16, 8, 128), F32),
            pltpu.VMEM((frames + 8, 128), F32),
            pltpu.VMEM((frames + 8, 128), F32),
            pltpu.VMEM((2, 16, 128), F32),
            pltpu.VMEM((2, 8, 128), F32),
            pltpu.VMEM((128, 128), F32),
            pltpu.VMEM((span, n_taps * mels), BF16),
            pltpu.VMEM((128, 128 * k_taps), BF16),
            pltpu.VMEM((2, span, half), BF16),
            pltpu.VMEM((4 * frames, 384 * k_taps), BF16),
            pltpu.VMEM((4 * frames, outs), F32),
            dma((13,)), dma, dma,
            dma((n,)), dma((n,)), dma((n,)), dma((n,)),
            dma((5,)), dma((5,)), dma((5,)), dma((5,)),
            dma((n_tm,)), dma((n_tm,)), dma((n_tm,)), dma, dma,
        ],
        compiler_params=pltpu.CompilerParams(
            collective_id=0, has_side_effects=True, vmem_limit_bytes=56 * 2**20
        ),
        cost_estimate=pl.CostEstimate(
            flops=2 * 9 * bins * frames * chans * chans, bytes_accessed=15 * 2**20, transcendentals=0
        ),
    )(*operands)


def solution(mesh):
    in_specs = (
        P(None, "freq", ("song", "tm")),
        P("freq", ("song", "tm")),
        P("song"),
        P(),
        P(),
        P(),
        P(),
        P(),
        P(),
        P(),
        P(),
        P("tm", None, None),
        P(),
        P(None, None, "freq"),
        P("freq"),
    )
    out_specs = (P("freq", ("song", "tm")), P("freq", ("song", "tm")))
    return jax.shard_map(shards, mesh=mesh, in_specs=in_specs, out_specs=out_specs, check_vma=False)
```

```python
import functools

import jax
import jax.numpy as jnp
from jax import lax
from jax.experimental import pallas as pl
from jax.experimental.pallas import tpu as pltpu
from jax.sharding import PartitionSpec as P

GROUPS = 32
EPSILON = 1e-05
STEP_SIZE = 0.25
MESH = pl.DeviceIdType.MESH
F32 = jnp.float32
BF16 = jnp.bfloat16
NT = (((1,), (1,)), ((), ()))


def dot(a, b):
    return jnp.dot(a, b, preferred_element_type=F32)


def dot_nt(a, b):
    return lax.dot_general(a, b, NT, preferred_element_type=F32)


def three_parts(x):
    hi = x.astype(BF16)
    rest = x - hi.astype(F32)
    mid = rest.astype(BF16)
    low = (rest - mid.astype(F32)).astype(BF16)
    return hi, mid, low


def block_kernel(
    n_tm, n_f, fused,
    lat_h, mel_h, tshift_h, gain1_h, shift1_h, w1_h, gain2_h, shift2_h, w2_h, bias2_h, proj_h,
    pre_h, pre_bias_h, up_h, up_bias_h,
    mel_out, vocal,
    lat, mel, tshift, gain1, shift1, w1, gain2, shift2, w2, bias2, proj, pre_bias, up_bias,
    pre, up,
    stats1, stats2, stage_l, stage_r, halo_l, halo_r, halo_b, corner_l, corner_r,
    act_l, act_r, spread, first, gpad, zt, z_part, z_before, z_after, turned,
    taps_in, repeat, feats, wide_f, acc,
    in_sem, up_sem, own_sem,
    s1_send, s1_recv, s2_send, s2_recv, h_send, h_recv, z_send, z_recv,
    p_send, p_recv, fw_send, ft_send, ft_recv,
):
    bins, frames, chans = lat.shape
    n = n_tm * n_f
    tm = lax.axis_index("tm")
    f = lax.axis_index("freq")
    me = tm * n_f + f
    other = 1 - f
    has_left = tm > 0
    has_right = tm < n_tm - 1

    def peer_of(k):
        p = lax.rem(me + k, n)
        return p, {"tm": p // n_f, "freq": lax.rem(p, n_f)}

    barrier = pltpu.get_barrier_semaphore()
    loads = [
        pltpu.make_async_copy(src, dst, in_sem.at[i])
        for i, (src, dst) in enumerate([
            (lat_h, lat), (w2_h, w2), (w1_h, w1), (mel_h, mel), (tshift_h, tshift), (gain1_h, gain1),
            (shift1_h, shift1), (gain2_h, gain2), (shift2_h, shift2), (bias2_h, bias2), (proj_h, proj),
            (pre_bias_h, pre_bias), (up_bias_h, up_bias),
        ])
    ]

    def greet(k, c):
        pl.semaphore_signal(barrier, inc=1, device_id=peer_of(k)[1], device_id_type=MESH)
        return c

    lax.fori_loop(1, n, greet, 0)
    for c in loads:
        c.start()
    loads[0].wait()
    load_up = pltpu.make_async_copy(up_h, up, up_sem)
    load_up.start()

    sub8 = lax.broadcasted_iota(jnp.int32, (bins, 8, chans), 1)
    head = lat[:, 0:16, :].astype(F32)[:, 0:8, :]
    tail = lat[:, frames - 16 : frames, :].astype(F32)[:, 8:16, :]
    stage_l[...] = jnp.sum(jnp.where(sub8 == 0, head, 0.0), axis=1).astype(BF16)
    stage_r[...] = jnp.sum(jnp.where(sub8 == 7, tail, 0.0), axis=1).astype(BF16)

    pl.semaphore_wait(barrier, n - 1)

    def remote(src, dst, send, recv, to):
        return pltpu.make_async_remote_copy(
            src_ref=src, dst_ref=dst, send_sem=send, recv_sem=recv, device_id=to, device_id_type=MESH
        )

    edge = pl.multiple_of((1 - f) * (bins - 16), 16)
    to_left = [{"tm": tm - 1, "freq": f}, {"tm": tm - 1, "freq": other}]
    to_right = [{"tm": tm + 1, "freq": f}, {"tm": tm + 1, "freq": other}]
    partner = {"tm": tm, "freq": other}
    h_bin = remote(lat.at[(1 - f) * (bins - 1)], halo_b, h_send.at[0], h_recv.at[0], partner)
    h_bin.start()
    go_left = [
        remote(stage_l, halo_r, h_send.at[1], h_recv.at[1], to_left[0]),
        remote(stage_l.at[pl.ds(edge, 16)], corner_r, h_send.at[2], h_recv.at[2], to_left[1]),
    ]
    go_right = [
        remote(stage_r, halo_l, h_send.at[3], h_recv.at[3], to_right[0]),
        remote(stage_r.at[pl.ds(edge, 16)], corner_l, h_send.at[4], h_recv.at[4], to_right[1]),
    ]

    @pl.when(has_left)
    def _():
        for c in go_left:
            c.start()

    @pl.when(has_right)
    def _():
        for c in go_right:
            c.start()

    def fold(x):
        return jnp.sum(x.reshape(-1, 8, chans), axis=0)

    def stat_step(b, carry):
        s, q = carry
        x = lat[pl.ds(b * 4, 4)].astype(F32)
        return s + fold(x), q + fold(x * x)

    zero8 = jnp.zeros((8, chans), F32)
    s, q = lax.fori_loop(0, bins // 4, stat_step, (zero8, zero8))

    def send_stats(s, q, stats, send, recv):
        stats[me] = jnp.concatenate(
            [jnp.sum(s, axis=0, keepdims=True), jnp.sum(q, axis=0, keepdims=True)], axis=1
        )

        def go(k, c):
            _, to = peer_of(k)
            remote(stats.at[me], stats.at[me], send.at[k], recv.at[me], to).start()
            return c

        lax.fori_loop(1, n, go, 0)

    def take_stats(stats, send, recv):
        def wait(k, c):
            p, to = peer_of(k)
            remote(stats.at[me], stats.at[p], send.at[k], recv.at[p], to).wait_recv()
            return c

        lax.fori_loop(1, n, wait, 0)
        total = jnp.sum(stats[...], axis=0)
        both = jnp.concatenate(
            [
                jnp.broadcast_to(total[:, :chans], (8, chans)),
                jnp.broadcast_to(total[:, chans:], (8, chans)),
            ],
            axis=0,
        )
        size = chans // GROUPS
        gi = lax.broadcasted_iota(jnp.int32, (chans, chans), 0) // size
        gj = lax.broadcasted_iota(jnp.int32, (chans, chans), 1) // size
        same = (gi == gj).astype(F32)
        sums = jnp.dot(both, same, preferred_element_type=F32, precision=lax.Precision.HIGHEST)
        count = float(size * bins * frames * n)
        mean = sums[0:1] / count
        var = sums[8:9] / count - mean * mean
        return mean, lax.rsqrt(var + EPSILON)

    def end_stats(stats, send, recv):
        def wait(k, c):
            p, to = peer_of(k)
            remote(stats.at[me], stats.at[me], send.at[k], recv.at[me], to).wait_send()
            return c

        lax.fori_loop(1, n, wait, 0)

    send_stats(s, q, stats1, s1_send, s1_recv)

    half_n = n_tm // n_f
    slot = lax.rem(tm, half_n)
    beside = tm + 1 - 2 * lax.rem(tm, 2)
    holder = f == tm // half_n

    def push(k):
        to = jnp.where(k == 0, beside, lax.rem(tm + 2 * k, n_tm))
        return remote(pre_h, pre.at[:, slot], p_send.at[k], p_recv.at[slot], {"tm": to, "freq": f})

    def forward(j):
        d = 2 * j + lax.rem(tm, 2)
        return d, remote(pre.at[:, d], pre.at[:, d], fw_send.at[j], p_recv.at[d], {"tm": beside, "freq": f})

    if fused:
        own_pre = pltpu.make_async_copy(pre_h, pre.at[:, slot], own_sem)
    else:
        own_pre = pltpu.make_async_copy(pre_h, pre, own_sem)
        own_pre.start()

    def gather_start():
        @pl.when(holder)
        def _():
            own_pre.start()

            def go(k, c):
                push(k).start()
                return c

            lax.fori_loop(0, n_tm // 2, go, 0)

    def gather_forward():
        def go(j, c):
            d, copy = forward(j)

            @pl.when(d + f * half_n != tm)
            def _():
                copy.wait_recv()
                copy.start()

            return c

        lax.fori_loop(0, half_n // 2, go, 0)

    def gather_end():
        @pl.when(holder)
        def _():
            own_pre.wait()

            def wait(k, c):
                push(k).wait_send()
                return c

            lax.fori_loop(0, n_tm // 2, wait, 0)

        def rest(j, c):
            d, copy = forward(j)

            @pl.when(d + f * half_n != tm)
            def _():
                copy.wait_send()

            e = 2 * j + 1 - lax.rem(tm, 2)
            remote(pre.at[:, e], pre.at[:, e], fw_send.at[j], p_recv.at[e], {"tm": beside, "freq": f}).wait_recv()
            return c

        lax.fori_loop(0, half_n // 2, rest, 0)

    if fused:
        gather_start()

    for c in loads[1:]:
        c.wait()

    k_taps = repeat.shape[1] // 128
    r = lax.broadcasted_iota(jnp.int32, repeat.shape, 0)
    c = lax.broadcasted_iota(jnp.int32, repeat.shape, 1)
    repeat[...] = (c // k_taps == r).astype(F32).astype(BF16)
    acc[...] = jnp.zeros(acc.shape, F32)
    gpad[...] = jnp.zeros(gpad.shape, F32)

    p_row = proj[...]
    hi, mid, low = [x.astype(F32) for x in three_parts(p_row)]
    row = lax.broadcasted_iota(jnp.int32, (16, chans), 0)
    parts = jnp.where(row == 0, hi, jnp.where(row == 1, mid, jnp.where(row == 2, low, 0.0))).astype(BF16)
    row24 = lax.broadcasted_iota(jnp.int32, (32, chans), 0)
    taps = jnp.zeros((32, chans), F32)
    for i in range(3):
        for j in range(3):
            wv = jnp.sum(dot_nt(parts, w2[3 * i + j]), axis=0, keepdims=True)
            a, b, _ = three_parts(wv)
            taps = jnp.where(row24 == 8 * j + i, a.astype(F32), taps)
            taps = jnp.where(row24 == 8 * j + 3 + i, b.astype(F32), taps)
    taps = taps.astype(BF16)
    direct = jnp.where(row24 == 9, hi, jnp.where(row24 == 12, mid, jnp.where(row24 == 14, low, 0.0))).astype(BF16)
    const = jnp.sum(p_row * bias2[...], axis=1, keepdims=True)

    h_bin.wait()

    @pl.when(has_left)
    def _():
        for c in go_left:
            c.wait_send()
        for c in go_right:
            c.wait_recv()

    @pl.when(has_right)
    def _():
        for c in go_right:
            c.wait_send()
        for c in go_left:
            c.wait_recv()

    mean, inv = take_stats(stats1, s1_send, s1_recv)
    scale = inv * gain1[...]
    shift = shift1[...]

    def silu(x, mean, scale, shift):
        y = (x - mean) * scale + shift
        h = 0.5 * y
        return h + h * jnp.tanh(h)

    left_on = jnp.where(has_left, 1.0, 0.0).astype(F32)
    right_on = jnp.where(has_right, 1.0, 0.0).astype(F32)

    def edge_act(ref, present):
        x = ref[...].astype(F32)
        return jnp.where(present, silu(x, mean, scale, shift), 0.0)

    act_l[...] = edge_act(halo_l, has_left)
    act_r[...] = edge_act(halo_r, has_right)
    cl = edge_act(corner_l, has_left)
    cr = edge_act(corner_r, has_right)
    pick = f * 15
    r16 = lax.broadcasted_iota(jnp.int32, (16, chans), 0)
    cl = jnp.sum(jnp.where(r16 == pick, cl, 0.0), axis=0, keepdims=True)
    cr = jnp.sum(jnp.where(r16 == pick, cr, 0.0), axis=0, keepdims=True)
    rows = lax.broadcasted_iota(jnp.int32, (frames, chans), 0)

    def put(at, x, left, right):
        spread[at, :, 0:chans] = jnp.where(rows == 0, left, pltpu.roll(x, 1, 0)).astype(BF16)
        spread[at, :, chans : 2 * chans] = x.astype(BF16)
        spread[at, :, 2 * chans : 3 * chans] = jnp.where(
            rows == frames - 1, right, pltpu.roll(x, frames - 1, 0)
        ).astype(BF16)

    put((1 - f) * (bins + 1), silu(halo_b[...].astype(F32), mean, scale, shift), cl, cr)
    spread[f * (bins + 1)] = jnp.zeros(spread.shape[1:], BF16)

    nb = 8
    moved = tshift[...]

    def norm_bins(start, end):
        for at in range(start, min(end, bins)):
            x = silu(lat[at].astype(F32), mean, scale, shift)
            put(at + 1, x, act_l[at : at + 1, :], act_r[at : at + 1, :])

    s, q = zero8, zero8
    norm_bins(0, nb + 1)
    for b in range(0, bins, nb):
        part = jnp.concatenate(
            [spread[b + i : b + i + nb].reshape(nb * frames, 3 * chans) for i in range(3)], axis=1
        )
        out = (dot(part, w1[...]) + moved).astype(BF16)
        norm_bins(b + nb + 1, b + 2 * nb + 1)
        first[b : b + nb] = out.reshape(nb, frames, chans)
        x = out.astype(F32)
        s, q = s + fold(x), q + fold(x * x)
    end_stats(stats1, s1_send, s1_recv)
    send_stats(s, q, stats2, s2_send, s2_recv)

    if fused:
        gather_forward()
    vb = 4
    sub = lax.broadcasted_iota(jnp.int32, (8, frames), 0)

    def direct_step(b, c):
        raw = lat[pl.ds(b * vb, vb)].reshape(vb * frames, chans)
        g = dot_nt(direct, raw)
        for u in range(vb):
            at = b * vb + u
            own = mel[pl.ds(at, 1), :] * (1.0 / STEP_SIZE) + const
            piece = g[8:16, u * frames : (u + 1) * frames]
            gpad[1, at + 2, :, 0:frames] = jnp.where(sub == 7, own, piece)
        return c

    lax.fori_loop(0, bins // vb, direct_step, 0)
    mean2, inv2 = take_stats(stats2, s2_send, s2_recv)
    scale2 = inv2 * gain2[...]
    low2 = shift2[...]

    def tap_step(b, c):
        x = first[pl.ds(b * vb, vb)].reshape(vb * frames, chans).astype(F32)
        act = silu(x, mean2, scale2, low2).astype(BF16)
        g = dot_nt(taps, act)
        for u in range(vb):
            at = b * vb + u
            for j in range(3):
                piece = g[8 * j : 8 * j + 8, u * frames : (u + 1) * frames]
                if j == 1:
                    piece = piece + gpad[j, at + 2, :, 0:frames]
                gpad[j, at + 2, :, 0:frames] = piece
        return c

    lax.fori_loop(0, bins // vb, tap_step, 0, unroll=4)
    end_stats(stats2, s2_send, s2_recv)

    tall = bins + 8
    subs = lax.broadcasted_iota(jnp.int32, (tall, 8, 128), 1)
    total = jnp.zeros((tall, 128), F32)
    for j in range(3):
        comb = jnp.zeros((tall, 8, 128), F32)
        for i in range(3):
            mine = (subs == i) | (subs == i + 3)
            if i == 1:
                mine = mine | (subs >= 6)
            comb = jnp.where(mine, gpad[j, i : i + tall], comb)
        rowsum = jnp.sum(comb, axis=1)
        total = total + (pltpu.roll(rowsum, 2 - j, 1) if j < 2 else rowsum)
    z = jnp.concatenate([total * STEP_SIZE, jnp.zeros((128 - tall, 128), F32)], axis=0)
    wide = frames + 8
    zt[...] = jnp.transpose(z)[0:wide]

    top = frames - 8
    z_own = remote(zt, z_part, z_send.at[0], z_recv.at[0], partner)
    z_left = [
        remote(zt.at[pl.ds(0, 8)], z_after.at[0], z_send.at[1], z_recv.at[1], to_left[0]),
        remote(zt.at[pl.ds(0, 8)], z_after.at[1], z_send.at[2], z_recv.at[2], to_left[1]),
    ]
    z_right = [
        remote(zt.at[pl.ds(top, 16)], z_before.at[0], z_send.at[3], z_recv.at[3], to_right[0]),
        remote(zt.at[pl.ds(top, 16)], z_before.at[1], z_send.at[4], z_recv.at[4], to_right[1]),
    ]

    @pl.when(has_left)
    def _():
        for c in z_left:
            c.start()

    @pl.when(has_right)
    def _():
        for c in z_right:
            c.start()

    z_own.start()

    @pl.when(has_left)
    def _():
        for c in z_left:
            c.wait_send()
        for c in z_right:
            c.wait_recv()

    @pl.when(has_right)
    def _():
        for c in z_right:
            c.wait_send()
        for c in z_left:
            c.wait_recv()

    z_own.wait()

    def lane_place(mine, theirs):
        shape = mine.shape
        lane = lax.broadcasted_iota(jnp.int32, shape, 1)
        low = jnp.where(f == 0, mine, theirs)
        high = jnp.where(f == 0, theirs, mine)
        low = jnp.where(lane <= bins, pltpu.roll(low, 127, 1), 0.0)
        high = jnp.where(lane >= bins - 1, pltpu.roll(high, bins - 1, 1), 0.0)
        return low + high

    span = frames + 16
    center = lane_place(zt[...], z_part[...])
    before = jnp.where(has_left, lane_place(z_before[0], z_before[1]), 0.0)
    after = jnp.where(has_right, lane_place(z_after[0], z_after[1]), 0.0)
    big = jnp.concatenate([center, jnp.zeros((8, 128), F32)], axis=0)
    big = pltpu.roll(big, 7, 0)
    r_b = lax.broadcasted_iota(jnp.int32, (16, 128), 0)
    before = jnp.where(r_b >= 1, before, 0.0)
    before = jnp.concatenate([before, jnp.zeros((span - 16, 128), F32)], axis=0)
    before = pltpu.roll(before, span - 1, 0)
    after = jnp.concatenate([after, jnp.zeros((span - 8, 128), F32)], axis=0)
    after = pltpu.roll(after, frames + 7, 0)
    pos = lax.broadcasted_iota(jnp.int32, (span, 128), 0) - 8 + tm * frames
    whole = jnp.where((pos >= 0) & (pos < n_tm * frames), big + before + after, 0.0)
    turned[...] = jnp.transpose(
        jnp.concatenate([whole[8 : 8 + frames], jnp.zeros((128 - frames, 128), F32)], axis=0)
    )
    mel_out[...] = turned[pl.ds(pl.multiple_of(f * bins, 8), bins), 0:frames]

    m = whole.astype(BF16).astype(F32)
    n_taps, mels = pre.shape[0], pre.shape[-1]
    width = feats.shape[2]
    for k in range(n_taps):
        s = (n_taps // 2 - k) % span
        taps_in[:, k * mels : (k + 1) * mels] = (pltpu.roll(m, s, 0) if s else m).astype(BF16)
    if fused:
        gather_end()
    else:
        own_pre.wait()
    made = jnp.zeros((span, width), F32)
    for k in range(n_taps):
        made = made + dot_nt(taps_in[:, k * mels : (k + 1) * mels], pre[k].reshape(width, mels))
    pos = lax.broadcasted_iota(jnp.int32, (span, width), 0) - 8 + tm * frames
    made = made + jnp.concatenate(
        [pre_bias[pl.ds(f * (width // 128) + i, 1), :] for i in range(width // 128)], axis=1
    )
    feats[f] = jnp.where((pos >= 0) & (pos < n_tm * frames), made, 0.0).astype(BF16)
    swap = remote(feats.at[f], feats.at[f], ft_send, ft_recv, partner)
    swap.start()
    load_up.wait()

    group = wide_f.shape[1] // k_taps
    rep = 128 * k_taps
    lane = lax.broadcasted_iota(jnp.int32, (span, rep), 1)
    upper = lax.rem(lane, k_taps) < 4
    phase = lax.rem(lane[0:frames], 4)

    def upsample(h):
        for g in range(width // group):
            for t in range(group // 128):
                at = g * group + t * 128
                wide = dot(feats[h, :, at : at + 128], repeat[...])
                wide = jnp.where(upper, wide, pltpu.roll(wide, 1, 0))
                for p in range(4):
                    start = 8 + (1 if p >= 2 else 0)
                    wide_f[p * frames : (p + 1) * frames, t * rep : (t + 1) * rep] = jnp.where(
                        phase == (p + 2) % 4, wide[start : start + frames], 0.0
                    ).astype(BF16)
            row = pl.multiple_of((h * width + g * group) * k_taps, 128)
            acc[...] += dot(wide_f[...], up[pl.ds(row, group * k_taps), :])

    upsample(f)
    swap.wait()
    upsample(other)
    bias = jnp.concatenate([up_bias[i : i + 1, :] for i in range(up_bias.shape[0])], axis=1)
    done = acc[...] + bias
    r = lax.broadcasted_iota(jnp.int32, (4 * frames, 4 * frames), 0)
    c = lax.broadcasted_iota(jnp.int32, (4 * frames, 4 * frames), 1)
    perm = (r == lax.rem(c, 4) * frames + c // 4).astype(F32).astype(BF16)
    vocal[...] = dot(jnp.transpose(done).astype(BF16), perm).astype(BF16)


def finish_kernel(mel, vocal, mel_out, vocal_out, sems):
    copies = [
        pltpu.make_async_copy(mel, mel_out, sems.at[0]),
        pltpu.make_async_copy(vocal, vocal_out, sems.at[1]),
    ]
    for c in copies:
        c.start()
    for c in copies:
        c.wait()


def shards(
    latent, mel_noisy, time_shift, first_gain, first_shift, conv_first, second_gain,
    second_shift, conv_second, second_bias, out_proj, pre_weight, pre_bias, up_weight, up_bias,
):
    chans, bins, frames = latent.shape
    n_tm, n_f = lax.axis_size("tm"), lax.axis_size("freq")
    n = n_tm * n_f
    lat = jnp.transpose(latent, (1, 2, 0))
    vec = lambda v: v.reshape(1, -1)
    vmem = pl.BlockSpec(memory_space=pltpu.VMEM)
    hbm = pl.BlockSpec(memory_space=pl.ANY)
    span = frames + 16
    dma = pltpu.SemaphoreType.DMA
    pre = jnp.transpose(pre_weight, (1, 0, 2))
    n_taps, rows, mels = pre.shape
    k_taps, outs = up_weight.shape[1], up_weight.shape[2]
    half = n_tm * rows // n_f
    fused = rows % 16 == 0 and n_tm % 4 == 0
    if fused:
        held = (n_taps, n_tm // n_f, rows, mels)
    else:
        held = (n_taps, half, mels)
        pre = lax.all_gather(pre, "tm", axis=1, tiled=True)
        pre = lax.dynamic_slice_in_dim(pre, lax.axis_index("freq") * half, half, axis=1)
    operands = (
        lat, mel_noisy, vec(time_shift), vec(first_gain), vec(first_shift),
        conv_first.reshape(9 * chans, chans), vec(second_gain), vec(second_shift),
        conv_second.reshape(9, chans, chans), vec(second_bias), vec(out_proj),
        pre, pre_bias.reshape(-1, 128), up_weight.reshape(-1, outs),
        up_bias.reshape(-1, 128),
    )
    copies = [pltpu.VMEM(x.shape, x.dtype) for x in operands[:11] + (operands[12], operands[14])]
    results = pl.pallas_call(
        functools.partial(block_kernel, n_tm, n_f, fused),
        out_shape=(
            jax.ShapeDtypeStruct((bins, frames), F32),
            jax.ShapeDtypeStruct((outs, 4 * frames), BF16),
        ),
        in_specs=[hbm] * 15,
        out_specs=(vmem, vmem),
        scratch_shapes=copies + [
            pltpu.VMEM(held, BF16),
            pltpu.VMEM(operands[13].shape, BF16),
            pltpu.VMEM((n, 1, 2 * chans), F32),
            pltpu.VMEM((n, 1, 2 * chans), F32),
            pltpu.VMEM((bins, chans), BF16),
            pltpu.VMEM((bins, chans), BF16),
            pltpu.VMEM((bins, chans), BF16),
            pltpu.VMEM((bins, chans), BF16),
            pltpu.VMEM((frames, chans), BF16),
            pltpu.VMEM((16, chans), BF16),
            pltpu.VMEM((16, chans), BF16),
            pltpu.VMEM((bins, chans), F32),
            pltpu.VMEM((bins, chans), F32),
            pltpu.VMEM((bins + 2, frames, 3 * chans), BF16),
            pltpu.VMEM((bins, frames, chans), BF16),
            pltpu.VMEM((3, bins + 16, 8, 128), F32),
            pltpu.VMEM((frames + 8, 128), F32),
            pltpu.VMEM((frames + 8, 128), F32),
            pltpu.VMEM((2, 16, 128), F32),
            pltpu.VMEM((2, 8, 128), F32),
            pltpu.VMEM((128, 128), F32),
            pltpu.VMEM((span, n_taps * mels), BF16),
            pltpu.VMEM((128, 128 * k_taps), BF16),
            pltpu.VMEM((2, span, half), BF16),
            pltpu.VMEM((4 * frames, 384 * k_taps), BF16),
            pltpu.VMEM((4 * frames, outs), F32),
            dma((13,)), dma, dma,
            dma((n,)), dma((n,)), dma((n,)), dma((n,)),
            dma((5,)), dma((5,)), dma((5,)), dma((5,)),
            dma((n_tm,)), dma((n_tm,)), dma((n_tm,)), dma, dma,
        ],
        compiler_params=pltpu.CompilerParams(
            collective_id=0, has_side_effects=True, vmem_limit_bytes=56 * 2**20
        ),
        cost_estimate=pl.CostEstimate(
            flops=2 * 9 * bins * frames * chans * chans, bytes_accessed=15 * 2**20, transcendentals=0
        ),
    )(*operands)
    return pl.pallas_call(
        finish_kernel,
        out_shape=(
            jax.ShapeDtypeStruct((bins, frames), F32),
            jax.ShapeDtypeStruct((outs, 4 * frames), BF16),
        ),
        in_specs=[hbm] * 2,
        out_specs=(hbm, hbm),
        scratch_shapes=[dma((2,))],
    )(*results)


def solution(mesh):
    in_specs = (
        P(None, "freq", ("song", "tm")),
        P("freq", ("song", "tm")),
        P("song"),
        P(),
        P(),
        P(),
        P(),
        P(),
        P(),
        P(),
        P(),
        P("tm", None, None),
        P(),
        P(None, None, "freq"),
        P("freq"),
    )
    out_specs = (P("freq", ("song", "tm")), P("freq", ("song", "tm")))
    return jax.shard_map(shards, mesh=mesh, in_specs=in_specs, out_specs=out_specs, check_vma=False)
```

```python
import functools

import jax
import jax.numpy as jnp
from jax import lax
from jax.experimental import pallas as pl
from jax.experimental.pallas import tpu as pltpu
from jax.sharding import PartitionSpec as P

GROUPS = 32
EPSILON = 1e-05
STEP_SIZE = 0.25
MESH = pl.DeviceIdType.MESH
F32 = jnp.float32
BF16 = jnp.bfloat16
NT = (((1,), (1,)), ((), ()))


def dot(a, b):
    return jnp.dot(a, b, preferred_element_type=F32)


def dot_nt(a, b):
    return lax.dot_general(a, b, NT, preferred_element_type=F32)


def three_parts(x):
    hi = x.astype(BF16)
    rest = x - hi.astype(F32)
    mid = rest.astype(BF16)
    low = (rest - mid.astype(F32)).astype(BF16)
    return hi, mid, low


def block_kernel(
    n_tm, n_f, fused,
    lat_h, mel_h, tshift_h, gain1_h, shift1_h, w1_h, gain2_h, shift2_h, w2_h, bias2_h, proj_h,
    pre_h, pre_bias_h, up_h, up_bias_h,
    mel_out, vocal,
    lat, mel, tshift, gain1, shift1, w1, gain2, shift2, w2, bias2, proj, pre_bias, up_bias,
    pre, up,
    stats1, stats2, stage_l, stage_r, halo_l, halo_r, halo_b, corner_l, corner_r,
    act_l, act_r, spread, first, gpad, zt, z_part, z_before, z_after, turned,
    taps_in, repeat, feats, wide_f, acc,
    in_sem, up_sem, own_sem,
    s1_send, s1_recv, s2_send, s2_recv, h_send, h_recv, z_send, z_recv,
    p_send, p_recv, fw_send, ft_send, ft_recv,
):
    bins, frames, chans = lat.shape
    n = n_tm * n_f
    tm = lax.axis_index("tm")
    f = lax.axis_index("freq")
    me = tm * n_f + f
    other = 1 - f
    has_left = tm > 0
    has_right = tm < n_tm - 1

    def peer_of(k):
        p = lax.rem(me + k, n)
        return p, {"tm": p // n_f, "freq": lax.rem(p, n_f)}

    barrier = pltpu.get_barrier_semaphore()
    loads = [
        pltpu.make_async_copy(src, dst, in_sem.at[i])
        for i, (src, dst) in enumerate([
            (lat_h, lat), (w2_h, w2), (w1_h, w1), (mel_h, mel), (tshift_h, tshift), (gain1_h, gain1),
            (shift1_h, shift1), (gain2_h, gain2), (shift2_h, shift2), (bias2_h, bias2), (proj_h, proj),
            (pre_bias_h, pre_bias), (up_bias_h, up_bias),
        ])
    ]

    def greet(k, c):
        pl.semaphore_signal(barrier, inc=1, device_id=peer_of(k)[1], device_id_type=MESH)
        return c

    lax.fori_loop(1, n, greet, 0)
    song = lax.axis_index("song")
    beside = tm + 1 - 2 * lax.rem(tm, 2)
    across = [{"song": 1 - song, "tm": tm, "freq": f}, {"song": 1 - song, "tm": beside, "freq": f}]
    if fused:
        for to in across:
            pl.semaphore_signal(barrier, inc=1, device_id=to, device_id_type=MESH)
    for c in loads:
        c.start()
    loads[0].wait()
    load_up = pltpu.make_async_copy(up_h, up, up_sem)
    load_up.start()

    sub8 = lax.broadcasted_iota(jnp.int32, (bins, 8, chans), 1)
    head = lat[:, 0:16, :].astype(F32)[:, 0:8, :]
    tail = lat[:, frames - 16 : frames, :].astype(F32)[:, 8:16, :]
    stage_l[...] = jnp.sum(jnp.where(sub8 == 0, head, 0.0), axis=1).astype(BF16)
    stage_r[...] = jnp.sum(jnp.where(sub8 == 7, tail, 0.0), axis=1).astype(BF16)

    pl.semaphore_wait(barrier, n + 1 if fused else n - 1)

    def remote(src, dst, send, recv, to):
        return pltpu.make_async_remote_copy(
            src_ref=src, dst_ref=dst, send_sem=send, recv_sem=recv, device_id=to, device_id_type=MESH
        )

    edge = pl.multiple_of((1 - f) * (bins - 16), 16)
    to_left = [{"tm": tm - 1, "freq": f}, {"tm": tm - 1, "freq": other}]
    to_right = [{"tm": tm + 1, "freq": f}, {"tm": tm + 1, "freq": other}]
    partner = {"tm": tm, "freq": other}
    h_bin = remote(lat.at[(1 - f) * (bins - 1)], halo_b, h_send.at[0], h_recv.at[0], partner)
    h_bin.start()
    go_left = [
        remote(stage_l, halo_r, h_send.at[1], h_recv.at[1], to_left[0]),
        remote(stage_l.at[pl.ds(edge, 16)], corner_r, h_send.at[2], h_recv.at[2], to_left[1]),
    ]
    go_right = [
        remote(stage_r, halo_l, h_send.at[3], h_recv.at[3], to_right[0]),
        remote(stage_r.at[pl.ds(edge, 16)], corner_l, h_send.at[4], h_recv.at[4], to_right[1]),
    ]

    @pl.when(has_left)
    def _():
        for c in go_left:
            c.start()

    @pl.when(has_right)
    def _():
        for c in go_right:
            c.start()

    def fold(x):
        return jnp.sum(x.reshape(-1, 8, chans), axis=0)

    def stat_step(b, carry):
        s, q = carry
        x = lat[pl.ds(b * 4, 4)].astype(F32)
        return s + fold(x), q + fold(x * x)

    zero8 = jnp.zeros((8, chans), F32)
    s, q = lax.fori_loop(0, bins // 4, stat_step, (zero8, zero8))

    def send_stats(s, q, stats, send, recv):
        stats[me] = jnp.concatenate(
            [jnp.sum(s, axis=0, keepdims=True), jnp.sum(q, axis=0, keepdims=True)], axis=1
        )

        def go(k, c):
            _, to = peer_of(k)
            remote(stats.at[me], stats.at[me], send.at[k], recv.at[me], to).start()
            return c

        lax.fori_loop(1, n, go, 0)

    def take_stats(stats, send, recv):
        def wait(k, c):
            p, to = peer_of(k)
            remote(stats.at[me], stats.at[p], send.at[k], recv.at[p], to).wait_recv()
            return c

        lax.fori_loop(1, n, wait, 0)
        total = jnp.sum(stats[...], axis=0)
        both = jnp.concatenate(
            [
                jnp.broadcast_to(total[:, :chans], (8, chans)),
                jnp.broadcast_to(total[:, chans:], (8, chans)),
            ],
            axis=0,
        )
        size = chans // GROUPS
        gi = lax.broadcasted_iota(jnp.int32, (chans, chans), 0) // size
        gj = lax.broadcasted_iota(jnp.int32, (chans, chans), 1) // size
        same = (gi == gj).astype(F32)
        sums = jnp.dot(both, same, preferred_element_type=F32, precision=lax.Precision.HIGHEST)
        count = float(size * bins * frames * n)
        mean = sums[0:1] / count
        var = sums[8:9] / count - mean * mean
        return mean, lax.rsqrt(var + EPSILON)

    def end_stats(stats, send, recv):
        def wait(k, c):
            p, to = peer_of(k)
            remote(stats.at[me], stats.at[me], send.at[k], recv.at[me], to).wait_send()
            return c

        lax.fori_loop(1, n, wait, 0)

    send_stats(s, q, stats1, s1_send, s1_recv)

    half_n = n_tm // n_f
    slot = lax.rem(tm, half_n)
    holder = f == tm // half_n
    parity = lax.rem(tm, 2)
    part_rows = pre.shape[-2] // 2

    def piece_of(d, h):
        return pre.at[:, d, pl.ds(pl.multiple_of(h * part_rows, 16), part_rows)]

    def push(k, h):
        to = jnp.where(k == 0, beside, lax.rem(tm + 2 * k, n_tm))
        src = pre_h.at[:, pl.ds(pl.multiple_of(h * part_rows, 16), part_rows)]
        return remote(src, piece_of(slot, h), p_send.at[k, h], p_recv.at[slot, h], {"tm": to, "freq": f})

    def forwards(d):
        return [
            remote(piece_of(d, song), piece_of(d, song), fw_send.at[d, i], p_recv.at[d, song], to)
            for i, to in enumerate([{"tm": beside, "freq": f}] + across)
        ]

    def arrived(d, h):
        remote(piece_of(d, h), piece_of(d, h), fw_send.at[d, 0], p_recv.at[d, h], across[0]).wait_recv()

    if fused:
        own_pre = pltpu.make_async_copy(pre_h, pre.at[:, slot], own_sem)
    else:
        own_pre = pltpu.make_async_copy(pre_h, pre, own_sem)
        own_pre.start()

    def gather_start():
        @pl.when(holder)
        def _():
            own_pre.start()

            def go(k, c):
                push(k, song).start()
                return c

            lax.fori_loop(0, n_tm // 2, go, 0)
            push(0, 1 - song).start()

    def gather_forward():
        def go(j, c):
            d = 2 * j + parity

            @pl.when(d + f * half_n != tm)
            def _():
                arrived(d, song)
                for copy in forwards(d):
                    copy.start()

            return c

        lax.fori_loop(0, half_n // 2, go, 0)

    def gather_end():
        @pl.when(holder)
        def _():
            own_pre.wait()

            def wait(k, c):
                push(k, song).wait_send()
                return c

            lax.fori_loop(0, n_tm // 2, wait, 0)
            push(0, 1 - song).wait_send()

        def rest(j, c):
            d = 2 * j + parity

            @pl.when(d + f * half_n != tm)
            def _():
                arrived(d, 1 - song)
                for copy in forwards(d):
                    copy.wait_send()

            e = 2 * j + 1 - parity
            arrived(e, 0)
            arrived(e, 1)
            return c

        lax.fori_loop(0, half_n // 2, rest, 0)

    if fused:
        gather_start()

    for c in loads[1:]:
        c.wait()

    acc[...] = jnp.zeros(acc.shape, F32)
    gpad[...] = jnp.zeros(gpad.shape, F32)

    p_row = proj[...]
    hi, mid, low = [x.astype(F32) for x in three_parts(p_row)]
    row = lax.broadcasted_iota(jnp.int32, (16, chans), 0)
    parts = jnp.where(row == 0, hi, jnp.where(row == 1, mid, jnp.where(row == 2, low, 0.0))).astype(BF16)
    row24 = lax.broadcasted_iota(jnp.int32, (32, chans), 0)
    taps = jnp.zeros((32, chans), F32)
    for i in range(3):
        for j in range(3):
            wv = jnp.sum(dot_nt(parts, w2[3 * i + j]), axis=0, keepdims=True)
            a, b, _ = three_parts(wv)
            taps = jnp.where(row24 == 8 * j + i, a.astype(F32), taps)
            taps = jnp.where(row24 == 8 * j + 3 + i, b.astype(F32), taps)
    taps = taps.astype(BF16)
    direct = jnp.where(row24 == 9, hi, jnp.where(row24 == 12, mid, jnp.where(row24 == 14, low, 0.0))).astype(BF16)
    const = jnp.sum(p_row * bias2[...], axis=1, keepdims=True)

    h_bin.wait()

    @pl.when(has_left)
    def _():
        for c in go_left:
            c.wait_send()
        for c in go_right:
            c.wait_recv()

    @pl.when(has_right)
    def _():
        for c in go_right:
            c.wait_send()
        for c in go_left:
            c.wait_recv()

    mean, inv = take_stats(stats1, s1_send, s1_recv)
    scale = inv * gain1[...]
    shift = shift1[...]

    def silu(x, mean, scale, shift):
        y = (x - mean) * scale + shift
        h = 0.5 * y
        return h + h * jnp.tanh(h)

    left_on = jnp.where(has_left, 1.0, 0.0).astype(F32)
    right_on = jnp.where(has_right, 1.0, 0.0).astype(F32)

    def edge_act(ref, present):
        x = ref[...].astype(F32)
        return jnp.where(present, silu(x, mean, scale, shift), 0.0)

    act_l[...] = edge_act(halo_l, has_left)
    act_r[...] = edge_act(halo_r, has_right)
    cl = edge_act(corner_l, has_left)
    cr = edge_act(corner_r, has_right)
    pick = f * 15
    r16 = lax.broadcasted_iota(jnp.int32, (16, chans), 0)
    cl = jnp.sum(jnp.where(r16 == pick, cl, 0.0), axis=0, keepdims=True)
    cr = jnp.sum(jnp.where(r16 == pick, cr, 0.0), axis=0, keepdims=True)
    rows = lax.broadcasted_iota(jnp.int32, (frames, chans), 0)

    def put(at, x, left, right):
        spread[at, :, 0:chans] = jnp.where(rows == 0, left, pltpu.roll(x, 1, 0)).astype(BF16)
        spread[at, :, chans : 2 * chans] = x.astype(BF16)
        spread[at, :, 2 * chans : 3 * chans] = jnp.where(
            rows == frames - 1, right, pltpu.roll(x, frames - 1, 0)
        ).astype(BF16)

    put((1 - f) * (bins + 1), silu(halo_b[...].astype(F32), mean, scale, shift), cl, cr)
    spread[f * (bins + 1)] = jnp.zeros(spread.shape[1:], BF16)

    nb = 8
    moved = tshift[...]

    def norm_bins(start, end):
        for at in range(start, min(end, bins)):
            x = silu(lat[at].astype(F32), mean, scale, shift)
            put(at + 1, x, act_l[at : at + 1, :], act_r[at : at + 1, :])

    s, q = zero8, zero8
    norm_bins(0, nb + 1)
    for b in range(0, bins, nb):
        part = jnp.concatenate(
            [spread[b + i : b + i + nb].reshape(nb * frames, 3 * chans) for i in range(3)], axis=1
        )
        out = (dot(part, w1[...]) + moved).astype(BF16)
        norm_bins(b + nb + 1, b + 2 * nb + 1)
        if fused and b == nb * (bins // nb // 2):
            gather_forward()
        first[b : b + nb] = out.reshape(nb, frames, chans)
        x = out.astype(F32)
        s, q = s + fold(x), q + fold(x * x)
    end_stats(stats1, s1_send, s1_recv)
    send_stats(s, q, stats2, s2_send, s2_recv)

    vb = 4
    sub = lax.broadcasted_iota(jnp.int32, (8, frames), 0)

    def direct_step(b, c):
        raw = lat[pl.ds(b * vb, vb)].reshape(vb * frames, chans)
        g = dot_nt(direct, raw)
        for u in range(vb):
            at = b * vb + u
            own = mel[pl.ds(at, 1), :] * (1.0 / STEP_SIZE) + const
            piece = g[8:16, u * frames : (u + 1) * frames]
            gpad[1, at + 2, :, 0:frames] = jnp.where(sub == 7, own, piece)
        return c

    lax.fori_loop(0, bins // vb, direct_step, 0)

    k_taps = repeat.shape[2] // 256
    r = lax.broadcasted_iota(jnp.int32, repeat.shape[1:], 0)
    c = lax.broadcasted_iota(jnp.int32, repeat.shape[1:], 1)
    tap = lax.rem(c, k_taps)
    chan = lax.rem(c // k_taps, 128)
    hit = r == jnp.where(tap >= 4, chan + 128, chan)
    turn = lax.rem(tap, 4) - c // (128 * k_taps)
    repeat[0] = jnp.where(hit & (turn == 2), 1.0, 0.0).astype(BF16)
    repeat[1] = jnp.where(hit & (turn == 0), 1.0, 0.0).astype(BF16)
    mean2, inv2 = take_stats(stats2, s2_send, s2_recv)
    scale2 = inv2 * gain2[...]
    low2 = shift2[...]

    def tap_step(b, c):
        x = first[pl.ds(b * vb, vb)].reshape(vb * frames, chans).astype(F32)
        act = silu(x, mean2, scale2, low2).astype(BF16)
        g = dot_nt(taps, act)
        for u in range(vb):
            at = b * vb + u
            for j in range(3):
                piece = g[8 * j : 8 * j + 8, u * frames : (u + 1) * frames]
                if j == 1:
                    piece = piece + gpad[j, at + 2, :, 0:frames]
                gpad[j, at + 2, :, 0:frames] = piece
        return c

    lax.fori_loop(0, bins // vb, tap_step, 0, unroll=4)
    end_stats(stats2, s2_send, s2_recv)

    tall = bins + 8
    subs = lax.broadcasted_iota(jnp.int32, (tall, 8, 128), 1)
    total = jnp.zeros((tall, 128), F32)
    for j in range(3):
        comb = jnp.zeros((tall, 8, 128), F32)
        for i in range(3):
            mine = (subs == i) | (subs == i + 3)
            if i == 1:
                mine = mine | (subs >= 6)
            comb = jnp.where(mine, gpad[j, i : i + tall], comb)
        rowsum = jnp.sum(comb, axis=1)
        total = total + (pltpu.roll(rowsum, 2 - j, 1) if j < 2 else rowsum)
    z = jnp.concatenate([total * STEP_SIZE, jnp.zeros((128 - tall, 128), F32)], axis=0)
    wide = frames + 8
    zt[...] = jnp.transpose(z)[0:wide]

    top = frames - 8
    z_own = remote(zt, z_part, z_send.at[0], z_recv.at[0], partner)
    z_left = [
        remote(zt.at[pl.ds(0, 8)], z_after.at[0], z_send.at[1], z_recv.at[1], to_left[0]),
        remote(zt.at[pl.ds(0, 8)], z_after.at[1], z_send.at[2], z_recv.at[2], to_left[1]),
    ]
    z_right = [
        remote(zt.at[pl.ds(top, 16)], z_before.at[0], z_send.at[3], z_recv.at[3], to_right[0]),
        remote(zt.at[pl.ds(top, 16)], z_before.at[1], z_send.at[4], z_recv.at[4], to_right[1]),
    ]

    @pl.when(has_left)
    def _():
        for c in z_left:
            c.start()

    @pl.when(has_right)
    def _():
        for c in z_right:
            c.start()

    z_own.start()

    @pl.when(has_left)
    def _():
        for c in z_left:
            c.wait_send()
        for c in z_right:
            c.wait_recv()

    @pl.when(has_right)
    def _():
        for c in z_right:
            c.wait_send()
        for c in z_left:
            c.wait_recv()

    z_own.wait()

    def lane_place(mine, theirs):
        shape = mine.shape
        lane = lax.broadcasted_iota(jnp.int32, shape, 1)
        low = jnp.where(f == 0, mine, theirs)
        high = jnp.where(f == 0, theirs, mine)
        low = jnp.where(lane <= bins, pltpu.roll(low, 127, 1), 0.0)
        high = jnp.where(lane >= bins - 1, pltpu.roll(high, bins - 1, 1), 0.0)
        return low + high

    span = frames + 16
    center = lane_place(zt[...], z_part[...])
    before = jnp.where(has_left, lane_place(z_before[0], z_before[1]), 0.0)
    after = jnp.where(has_right, lane_place(z_after[0], z_after[1]), 0.0)
    big = jnp.concatenate([center, jnp.zeros((8, 128), F32)], axis=0)
    big = pltpu.roll(big, 7, 0)
    r_b = lax.broadcasted_iota(jnp.int32, (16, 128), 0)
    before = jnp.where(r_b >= 1, before, 0.0)
    before = jnp.concatenate([before, jnp.zeros((span - 16, 128), F32)], axis=0)
    before = pltpu.roll(before, span - 1, 0)
    after = jnp.concatenate([after, jnp.zeros((span - 8, 128), F32)], axis=0)
    after = pltpu.roll(after, frames + 7, 0)
    pos = lax.broadcasted_iota(jnp.int32, (span, 128), 0) - 8 + tm * frames
    whole = jnp.where((pos >= 0) & (pos < n_tm * frames), big + before + after, 0.0)
    turned[...] = jnp.transpose(
        jnp.concatenate([whole[8 : 8 + frames], jnp.zeros((128 - frames, 128), F32)], axis=0)
    )
    mel_out[...] = turned[pl.ds(pl.multiple_of(f * bins, 8), bins), 0:frames]

    m = whole.astype(BF16).astype(F32)
    n_taps, mels = pre.shape[0], pre.shape[-1]
    width = feats.shape[2]
    for k in range(n_taps):
        s = (n_taps // 2 - k) % span
        taps_in[:, k * mels : (k + 1) * mels] = (pltpu.roll(m, s, 0) if s else m).astype(BF16)
    if fused:
        gather_end()
    else:
        own_pre.wait()
    made = jnp.zeros((span, width), F32)
    for k in range(n_taps):
        made = made + dot_nt(taps_in[:, k * mels : (k + 1) * mels], pre[k].reshape(width, mels))
    pos = lax.broadcasted_iota(jnp.int32, (span, width), 0) - 8 + tm * frames
    made = made + jnp.concatenate(
        [pre_bias[pl.ds(f * (width // 128) + i, 1), :] for i in range(width // 128)], axis=1
    )
    feats[f] = jnp.where((pos >= 0) & (pos < n_tm * frames), made, 0.0).astype(BF16)
    swap = remote(feats.at[f], feats.at[f], ft_send, ft_recv, partner)
    swap.start()
    load_up.wait()

    group = wide_f.shape[1] // k_taps
    rep = 128 * k_taps

    def upsample(h):
        x = feats[h].astype(F32)
        mid = x[8 : 8 + frames].astype(BF16)
        prev = pltpu.roll(x, 1, 0)[8 : 8 + frames].astype(BF16)
        later = pltpu.roll(x, span - 1, 0)[8 : 8 + frames].astype(BF16)
        for g in range(width // group):
            for t in range(group // 128):
                cols = slice(g * group + t * 128, g * group + t * 128 + 128)
                for half_of, pair in enumerate(((mid, prev), (later, mid))):
                    both = jnp.concatenate([v[:, cols] for v in pair], axis=1)
                    wide = dot(both, repeat[half_of]).astype(BF16)
                    for p in range(2):
                        top = (2 * half_of + p) * frames
                        wide_f[top : top + frames, t * rep : (t + 1) * rep] = wide[:, p * rep : (p + 1) * rep]
            row = pl.multiple_of((h * width + g * group) * k_taps, 128)
            acc[...] += dot(wide_f[...], up[pl.ds(row, group * k_taps), :])

    upsample(f)
    swap.wait()
    upsample(other)
    bias = jnp.concatenate([up_bias[i : i + 1, :] for i in range(up_bias.shape[0])], axis=1)
    done = acc[...] + bias
    r = lax.broadcasted_iota(jnp.int32, (4 * frames, 4 * frames), 0)
    c = lax.broadcasted_iota(jnp.int32, (4 * frames, 4 * frames), 1)
    perm = (r == lax.rem(c, 4) * frames + c // 4).astype(F32).astype(BF16)
    vocal[...] = dot(jnp.transpose(done).astype(BF16), perm).astype(BF16)


def shards(
    latent, mel_noisy, time_shift, first_gain, first_shift, conv_first, second_gain,
    second_shift, conv_second, second_bias, out_proj, pre_weight, pre_bias, up_weight, up_bias,
):
    chans, bins, frames = latent.shape
    n_tm, n_f = lax.axis_size("tm"), lax.axis_size("freq")
    n = n_tm * n_f
    lat = jnp.transpose(latent, (1, 2, 0))
    vec = lambda v: v.reshape(1, -1)
    vmem = pl.BlockSpec(memory_space=pltpu.VMEM)
    hbm = pl.BlockSpec(memory_space=pl.ANY)
    span = frames + 16
    dma = pltpu.SemaphoreType.DMA
    pre = jnp.transpose(pre_weight, (1, 0, 2))
    n_taps, rows, mels = pre.shape
    k_taps, outs = up_weight.shape[1], up_weight.shape[2]
    half = n_tm * rows // n_f
    fused = rows % 32 == 0 and n_tm % 4 == 0 and lax.axis_size("song") == 2
    if fused:
        held = (n_taps, n_tm // n_f, rows, mels)
    else:
        held = (n_taps, half, mels)
        pre = lax.all_gather(pre, "tm", axis=1, tiled=True)
        pre = lax.dynamic_slice_in_dim(pre, lax.axis_index("freq") * half, half, axis=1)
    operands = (
        lat, mel_noisy, vec(time_shift), vec(first_gain), vec(first_shift),
        conv_first.reshape(9 * chans, chans), vec(second_gain), vec(second_shift),
        conv_second.reshape(9, chans, chans), vec(second_bias), vec(out_proj),
        pre, pre_bias.reshape(-1, 128), up_weight.reshape(-1, outs),
        up_bias.reshape(-1, 128),
    )
    copies = [pltpu.VMEM(x.shape, x.dtype) for x in operands[:11] + (operands[12], operands[14])]
    return pl.pallas_call(
        functools.partial(block_kernel, n_tm, n_f, fused),
        out_shape=(
            jax.ShapeDtypeStruct((bins, frames), F32),
            jax.ShapeDtypeStruct((outs, 4 * frames), BF16),
        ),
        in_specs=[hbm] * 15,
        out_specs=(vmem, vmem),
        scratch_shapes=copies + [
            pltpu.VMEM(held, BF16),
            pltpu.VMEM(operands[13].shape, BF16),
            pltpu.VMEM((n, 1, 2 * chans), F32),
            pltpu.VMEM((n, 1, 2 * chans), F32),
            pltpu.VMEM((bins, chans), BF16),
            pltpu.VMEM((bins, chans), BF16),
            pltpu.VMEM((bins, chans), BF16),
            pltpu.VMEM((bins, chans), BF16),
            pltpu.VMEM((frames, chans), BF16),
            pltpu.VMEM((16, chans), BF16),
            pltpu.VMEM((16, chans), BF16),
            pltpu.VMEM((bins, chans), F32),
            pltpu.VMEM((bins, chans), F32),
            pltpu.VMEM((bins + 2, frames, 3 * chans), BF16),
            pltpu.VMEM((bins, frames, chans), BF16),
            pltpu.VMEM((3, bins + 16, 8, 128), F32),
            pltpu.VMEM((frames + 8, 128), F32),
            pltpu.VMEM((frames + 8, 128), F32),
            pltpu.VMEM((2, 16, 128), F32),
            pltpu.VMEM((2, 8, 128), F32),
            pltpu.VMEM((128, 128), F32),
            pltpu.VMEM((span, n_taps * mels), BF16),
            pltpu.VMEM((2, 256, 256 * k_taps), BF16),
            pltpu.VMEM((2, span, half), BF16),
            pltpu.VMEM((4 * frames, 384 * k_taps), BF16),
            pltpu.VMEM((4 * frames, outs), F32),
            dma((13,)), dma, dma,
            dma((n,)), dma((n,)), dma((n,)), dma((n,)),
            dma((5,)), dma((5,)), dma((5,)), dma((5,)),
            dma((n_tm // 2, 2)), dma((n_tm // 2, 2)), dma((n_tm // 2, 3)), dma, dma,
        ],
        compiler_params=pltpu.CompilerParams(
            collective_id=0, has_side_effects=True, vmem_limit_bytes=56 * 2**20
        ),
        cost_estimate=pl.CostEstimate(
            flops=2 * 9 * bins * frames * chans * chans, bytes_accessed=15 * 2**20, transcendentals=0
        ),
    )(*operands)


def solution(mesh):
    in_specs = (
        P(None, "freq", ("song", "tm")),
        P("freq", ("song", "tm")),
        P("song"),
        P(),
        P(),
        P(),
        P(),
        P(),
        P(),
        P(),
        P(),
        P("tm", None, None),
        P(),
        P(None, None, "freq"),
        P("freq"),
    )
    out_specs = (P("freq", ("song", "tm")), P("freq", ("song", "tm")))
    return jax.shard_map(shards, mesh=mesh, in_specs=in_specs, out_specs=out_specs, check_vma=False)
```

```python
import functools

import jax
import jax.numpy as jnp
from jax import lax
from jax.experimental import pallas as pl
from jax.experimental.pallas import tpu as pltpu
from jax.sharding import PartitionSpec as P

GROUPS = 32
EPSILON = 1e-05
STEP_SIZE = 0.25
MESH = pl.DeviceIdType.MESH
F32 = jnp.float32
BF16 = jnp.bfloat16
NT = (((1,), (1,)), ((), ()))


def dot(a, b):
    return jnp.dot(a, b, preferred_element_type=F32)


def dot_nt(a, b):
    return lax.dot_general(a, b, NT, preferred_element_type=F32)


def three_parts(x):
    hi = x.astype(BF16)
    rest = x - hi.astype(F32)
    mid = rest.astype(BF16)
    low = (rest - mid.astype(F32)).astype(BF16)
    return hi, mid, low


def block_kernel(
    n_tm, n_f, fused,
    lat_h, mel_h, tshift_h, gain1_h, shift1_h, w1_h, gain2_h, shift2_h, w2_h, bias2_h, proj_h,
    pre_h, pre_bias_h, up_h, up_bias_h,
    mel_out, vocal,
    lat, mel, tshift, gain1, shift1, w1, gain2, shift2, w2, bias2, proj, pre_bias, up_bias,
    pre, up,
    stats1, stats2, stage_l, stage_r, halo_l, halo_r, halo_b, corner_l, corner_r,
    act_l, act_r, spread, first, gpad, zt, z_part, z_before, z_after, turned,
    taps_in, repeat, feats, wide_f, acc,
    in_sem, up_sem, own_sem,
    s1_send, s1_recv, s2_send, s2_recv, h_send, h_recv, z_send, z_recv,
    p_send, p_recv, fw_send, ft_send, ft_recv,
):
    bins, frames, chans = lat.shape
    n = n_tm * n_f
    tm = lax.axis_index("tm")
    f = lax.axis_index("freq")
    me = tm * n_f + f
    other = 1 - f
    has_left = tm > 0
    has_right = tm < n_tm - 1

    def peer_of(k):
        p = lax.rem(me + k, n)
        return p, {"tm": p // n_f, "freq": lax.rem(p, n_f)}

    barrier = pltpu.get_barrier_semaphore()
    loads = [
        pltpu.make_async_copy(src, dst, in_sem.at[i])
        for i, (src, dst) in enumerate([
            (lat_h, lat), (w2_h, w2), (w1_h, w1), (mel_h, mel), (tshift_h, tshift), (gain1_h, gain1),
            (shift1_h, shift1), (gain2_h, gain2), (shift2_h, shift2), (bias2_h, bias2), (proj_h, proj),
            (pre_bias_h, pre_bias), (up_bias_h, up_bias),
        ])
    ]

    def greet(k, c):
        pl.semaphore_signal(barrier, inc=1, device_id=peer_of(k)[1], device_id_type=MESH)
        return c

    lax.fori_loop(1, n, greet, 0)
    song = lax.axis_index("song")
    beside = tm + 1 - 2 * lax.rem(tm, 2)
    across = [{"song": 1 - song, "tm": tm, "freq": f}, {"song": 1 - song, "tm": beside, "freq": f}]
    if fused:
        for to in across:
            pl.semaphore_signal(barrier, inc=1, device_id=to, device_id_type=MESH)
    for c in loads:
        c.start()
    acc[...] = jnp.zeros(acc.shape, F32)
    gpad[...] = jnp.zeros(gpad.shape, F32)

    k_taps = repeat.shape[2] // 256
    r = lax.broadcasted_iota(jnp.int32, repeat.shape[1:], 0)
    c = lax.broadcasted_iota(jnp.int32, (1, repeat.shape[2]), 1)
    tap = lax.rem(c, k_taps)
    chan = lax.rem(c // k_taps, 128)
    source = jnp.where(tap >= 4, chan + 128, chan)
    turn = lax.rem(tap, 4) - c // (128 * k_taps)
    for g in range(2):
        wanted = jnp.where(turn == 2 - 2 * g, source, -1)
        repeat[g] = jnp.where(r == wanted, 1.0, 0.0).astype(BF16)
    loads[0].wait()
    load_up = pltpu.make_async_copy(up_h, up, up_sem)
    load_up.start()

    sub8 = lax.broadcasted_iota(jnp.int32, (bins, 8, chans), 1)
    head = lat[:, 0:16, :].astype(F32)[:, 0:8, :]
    tail = lat[:, frames - 16 : frames, :].astype(F32)[:, 8:16, :]
    stage_l[...] = jnp.sum(jnp.where(sub8 == 0, head, 0.0), axis=1).astype(BF16)
    stage_r[...] = jnp.sum(jnp.where(sub8 == 7, tail, 0.0), axis=1).astype(BF16)

    pl.semaphore_wait(barrier, n + 1 if fused else n - 1)

    def remote(src, dst, send, recv, to):
        return pltpu.make_async_remote_copy(
            src_ref=src, dst_ref=dst, send_sem=send, recv_sem=recv, device_id=to, device_id_type=MESH
        )

    edge = pl.multiple_of((1 - f) * (bins - 16), 16)
    to_left = [{"tm": tm - 1, "freq": f}, {"tm": tm - 1, "freq": other}]
    to_right = [{"tm": tm + 1, "freq": f}, {"tm": tm + 1, "freq": other}]
    partner = {"tm": tm, "freq": other}
    h_bin = remote(lat.at[(1 - f) * (bins - 1)], halo_b, h_send.at[0], h_recv.at[0], partner)
    h_bin.start()
    go_left = [
        remote(stage_l, halo_r, h_send.at[1], h_recv.at[1], to_left[0]),
        remote(stage_l.at[pl.ds(edge, 16)], corner_r, h_send.at[2], h_recv.at[2], to_left[1]),
    ]
    go_right = [
        remote(stage_r, halo_l, h_send.at[3], h_recv.at[3], to_right[0]),
        remote(stage_r.at[pl.ds(edge, 16)], corner_l, h_send.at[4], h_recv.at[4], to_right[1]),
    ]

    @pl.when(has_left)
    def _():
        for c in go_left:
            c.start()

    @pl.when(has_right)
    def _():
        for c in go_right:
            c.start()

    def fold(x):
        return jnp.sum(x.reshape(-1, 8, chans), axis=0)

    def stat_step(b, carry):
        s, q = carry
        x = lat[pl.ds(b * 4, 4)].astype(F32)
        return s + fold(x), q + fold(x * x)

    zero8 = jnp.zeros((8, chans), F32)
    s, q = lax.fori_loop(0, bins // 4, stat_step, (zero8, zero8))

    def send_stats(s, q, stats, send, recv):
        stats[me] = jnp.concatenate(
            [jnp.sum(s, axis=0, keepdims=True), jnp.sum(q, axis=0, keepdims=True)], axis=1
        )

        def go(k, c):
            _, to = peer_of(k)
            remote(stats.at[me], stats.at[me], send.at[k], recv.at[me], to).start()
            return c

        lax.fori_loop(1, n, go, 0)

    def take_stats(stats, send, recv):
        def wait(k, c):
            p, to = peer_of(k)
            remote(stats.at[me], stats.at[p], send.at[k], recv.at[p], to).wait_recv()
            return c

        lax.fori_loop(1, n, wait, 0)
        total = jnp.sum(stats[...], axis=0)
        both = jnp.concatenate(
            [
                jnp.broadcast_to(total[:, :chans], (8, chans)),
                jnp.broadcast_to(total[:, chans:], (8, chans)),
            ],
            axis=0,
        )
        size = chans // GROUPS
        gi = lax.broadcasted_iota(jnp.int32, (chans, chans), 0) // size
        gj = lax.broadcasted_iota(jnp.int32, (chans, chans), 1) // size
        same = (gi == gj).astype(F32)
        sums = jnp.dot(both, same, preferred_element_type=F32, precision=lax.Precision.HIGHEST)
        count = float(size * bins * frames * n)
        mean = sums[0:1] / count
        var = sums[8:9] / count - mean * mean
        return mean, lax.rsqrt(var + EPSILON)

    def end_stats(stats, send, recv):
        def wait(k, c):
            p, to = peer_of(k)
            remote(stats.at[me], stats.at[me], send.at[k], recv.at[me], to).wait_send()
            return c

        lax.fori_loop(1, n, wait, 0)

    send_stats(s, q, stats1, s1_send, s1_recv)

    half_n = n_tm // n_f
    slot = lax.rem(tm, half_n)
    holder = f == tm // half_n
    parity = lax.rem(tm, 2)
    part_rows = pre.shape[-2] // 2

    def piece_of(d, h):
        return pre.at[:, d, pl.ds(pl.multiple_of(h * part_rows, 16), part_rows)]

    def push(k, h):
        to = jnp.where(k == 0, beside, lax.rem(tm + 2 * k, n_tm))
        src = pre_h.at[:, pl.ds(pl.multiple_of(h * part_rows, 16), part_rows)]
        return remote(src, piece_of(slot, h), p_send.at[k, h], p_recv.at[slot, h], {"tm": to, "freq": f})

    def forwards(d):
        return [
            remote(piece_of(d, song), piece_of(d, song), fw_send.at[d, i], p_recv.at[d, song], to)
            for i, to in enumerate([{"tm": beside, "freq": f}] + across)
        ]

    def arrived(d, h):
        remote(piece_of(d, h), piece_of(d, h), fw_send.at[d, 0], p_recv.at[d, h], across[0]).wait_recv()

    if fused:
        own_pre = pltpu.make_async_copy(pre_h, pre.at[:, slot], own_sem)
    else:
        own_pre = pltpu.make_async_copy(pre_h, pre, own_sem)
        own_pre.start()

    def gather_start():
        @pl.when(holder)
        def _():
            own_pre.start()

            def go(k, c):
                push(k, song).start()
                return c

            lax.fori_loop(0, n_tm // 2, go, 0)
            push(0, 1 - song).start()

    def gather_forward():
        def go(j, c):
            d = 2 * j + parity

            @pl.when(d + f * half_n != tm)
            def _():
                arrived(d, song)
                for copy in forwards(d):
                    copy.start()

            return c

        lax.fori_loop(0, half_n // 2, go, 0)

    def gather_end():
        @pl.when(holder)
        def _():
            own_pre.wait()

            def wait(k, c):
                push(k, song).wait_send()
                return c

            lax.fori_loop(0, n_tm // 2, wait, 0)
            push(0, 1 - song).wait_send()

        def rest(j, c):
            d = 2 * j + parity

            @pl.when(d + f * half_n != tm)
            def _():
                arrived(d, 1 - song)
                for copy in forwards(d):
                    copy.wait_send()

            e = 2 * j + 1 - parity
            arrived(e, 0)
            arrived(e, 1)
            return c

        lax.fori_loop(0, half_n // 2, rest, 0)

    if fused:
        gather_start()

    for c in loads[1:]:
        c.wait()


    p_row = proj[...]
    hi, mid, low = [x.astype(F32) for x in three_parts(p_row)]
    row = lax.broadcasted_iota(jnp.int32, (16, chans), 0)
    parts = jnp.where(row == 0, hi, jnp.where(row == 1, mid, jnp.where(row == 2, low, 0.0))).astype(BF16)
    row24 = lax.broadcasted_iota(jnp.int32, (32, chans), 0)
    taps = jnp.zeros((32, chans), F32)
    for i in range(3):
        for j in range(3):
            wv = jnp.sum(dot_nt(parts, w2[3 * i + j]), axis=0, keepdims=True)
            a, b, _ = three_parts(wv)
            taps = jnp.where(row24 == 8 * j + i, a.astype(F32), taps)
            taps = jnp.where(row24 == 8 * j + 3 + i, b.astype(F32), taps)
    taps = taps.astype(BF16)
    direct = jnp.where(row24 == 9, hi, jnp.where(row24 == 12, mid, jnp.where(row24 == 14, low, 0.0))).astype(BF16)
    const = jnp.sum(p_row * bias2[...], axis=1, keepdims=True)

    h_bin.wait()

    @pl.when(has_left)
    def _():
        for c in go_left:
            c.wait_send()
        for c in go_right:
            c.wait_recv()

    @pl.when(has_right)
    def _():
        for c in go_right:
            c.wait_send()
        for c in go_left:
            c.wait_recv()

    mean, inv = take_stats(stats1, s1_send, s1_recv)
    scale = inv * gain1[...]
    shift = shift1[...]

    def silu(x, mean, scale, shift):
        y = (x - mean) * scale + shift
        h = 0.5 * y
        return h + h * jnp.tanh(h)

    left_on = jnp.where(has_left, 1.0, 0.0).astype(F32)
    right_on = jnp.where(has_right, 1.0, 0.0).astype(F32)

    def edge_act(ref, present):
        x = ref[...].astype(F32)
        return jnp.where(present, silu(x, mean, scale, shift), 0.0)

    act_l[...] = edge_act(halo_l, has_left)
    act_r[...] = edge_act(halo_r, has_right)
    cl = edge_act(corner_l, has_left)
    cr = edge_act(corner_r, has_right)
    pick = f * 15
    r16 = lax.broadcasted_iota(jnp.int32, (16, chans), 0)
    cl = jnp.sum(jnp.where(r16 == pick, cl, 0.0), axis=0, keepdims=True)
    cr = jnp.sum(jnp.where(r16 == pick, cr, 0.0), axis=0, keepdims=True)
    rows = lax.broadcasted_iota(jnp.int32, (frames, chans), 0)

    def put(at, x, left, right):
        spread[at, :, 0:chans] = jnp.where(rows == 0, left, pltpu.roll(x, 1, 0)).astype(BF16)
        spread[at, :, chans : 2 * chans] = x.astype(BF16)
        spread[at, :, 2 * chans : 3 * chans] = jnp.where(
            rows == frames - 1, right, pltpu.roll(x, frames - 1, 0)
        ).astype(BF16)

    put((1 - f) * (bins + 1), silu(halo_b[...].astype(F32), mean, scale, shift), cl, cr)
    spread[f * (bins + 1)] = jnp.zeros(spread.shape[1:], BF16)

    nb = 8
    moved = tshift[...]

    def norm_bins(start, end):
        for at in range(start, min(end, bins)):
            x = silu(lat[at].astype(F32), mean, scale, shift)
            put(at + 1, x, act_l[at : at + 1, :], act_r[at : at + 1, :])

    s, q = zero8, zero8
    norm_bins(0, nb + 1)
    for b in range(0, bins, nb):
        part = jnp.concatenate(
            [spread[b + i : b + i + nb].reshape(nb * frames, 3 * chans) for i in range(3)], axis=1
        )
        out = (dot(part, w1[...]) + moved).astype(BF16)
        norm_bins(b + nb + 1, b + 2 * nb + 1)
        first[b : b + nb] = out.reshape(nb, frames, chans)
        x = out.astype(F32)
        s, q = s + fold(x), q + fold(x * x)
    end_stats(stats1, s1_send, s1_recv)
    send_stats(s, q, stats2, s2_send, s2_recv)

    if fused:
        gather_forward()
    vb = 4
    sub = lax.broadcasted_iota(jnp.int32, (8, frames), 0)

    def direct_step(b, c):
        raw = lat[pl.ds(b * vb, vb)].reshape(vb * frames, chans)
        g = dot_nt(direct, raw)
        for u in range(vb):
            at = b * vb + u
            own = mel[pl.ds(at, 1), :] * (1.0 / STEP_SIZE) + const
            piece = g[8:16, u * frames : (u + 1) * frames]
            gpad[1, at + 2, :, 0:frames] = jnp.where(sub == 7, own, piece)
        return c

    lax.fori_loop(0, bins // vb, direct_step, 0)

    mean2, inv2 = take_stats(stats2, s2_send, s2_recv)
    scale2 = inv2 * gain2[...]
    low2 = shift2[...]

    def tap_step(b, c):
        x = first[pl.ds(b * vb, vb)].reshape(vb * frames, chans).astype(F32)
        act = silu(x, mean2, scale2, low2).astype(BF16)
        g = dot_nt(taps, act)
        for u in range(vb):
            at = b * vb + u
            for j in range(3):
                piece = g[8 * j : 8 * j + 8, u * frames : (u + 1) * frames]
                if j == 1:
                    piece = piece + gpad[j, at + 2, :, 0:frames]
                gpad[j, at + 2, :, 0:frames] = piece
        return c

    lax.fori_loop(0, bins // vb, tap_step, 0, unroll=4)
    end_stats(stats2, s2_send, s2_recv)

    tall = bins + 8
    subs = lax.broadcasted_iota(jnp.int32, (tall, 8, 128), 1)
    total = jnp.zeros((tall, 128), F32)
    for j in range(3):
        comb = jnp.zeros((tall, 8, 128), F32)
        for i in range(3):
            mine = (subs == i) | (subs == i + 3)
            if i == 1:
                mine = mine | (subs >= 6)
            comb = jnp.where(mine, gpad[j, i : i + tall], comb)
        rowsum = jnp.sum(comb, axis=1)
        total = total + (pltpu.roll(rowsum, 2 - j, 1) if j < 2 else rowsum)
    z = jnp.concatenate([total * STEP_SIZE, jnp.zeros((128 - tall, 128), F32)], axis=0)
    wide = frames + 8
    zt[...] = jnp.transpose(z)[0:wide]

    top = frames - 8
    z_own = remote(zt, z_part, z_send.at[0], z_recv.at[0], partner)
    z_left = [
        remote(zt.at[pl.ds(0, 8)], z_after.at[0], z_send.at[1], z_recv.at[1], to_left[0]),
        remote(zt.at[pl.ds(0, 8)], z_after.at[1], z_send.at[2], z_recv.at[2], to_left[1]),
    ]
    z_right = [
        remote(zt.at[pl.ds(top, 16)], z_before.at[0], z_send.at[3], z_recv.at[3], to_right[0]),
        remote(zt.at[pl.ds(top, 16)], z_before.at[1], z_send.at[4], z_recv.at[4], to_right[1]),
    ]

    @pl.when(has_left)
    def _():
        for c in z_left:
            c.start()

    @pl.when(has_right)
    def _():
        for c in z_right:
            c.start()

    z_own.start()

    @pl.when(has_left)
    def _():
        for c in z_left:
            c.wait_send()
        for c in z_right:
            c.wait_recv()

    @pl.when(has_right)
    def _():
        for c in z_right:
            c.wait_send()
        for c in z_left:
            c.wait_recv()

    z_own.wait()

    def lane_place(mine, theirs):
        shape = mine.shape
        lane = lax.broadcasted_iota(jnp.int32, shape, 1)
        low = jnp.where(f == 0, mine, theirs)
        high = jnp.where(f == 0, theirs, mine)
        low = jnp.where(lane <= bins, pltpu.roll(low, 127, 1), 0.0)
        high = jnp.where(lane >= bins - 1, pltpu.roll(high, bins - 1, 1), 0.0)
        return low + high

    span = frames + 16
    center = lane_place(zt[...], z_part[...])
    before = jnp.where(has_left, lane_place(z_before[0], z_before[1]), 0.0)
    after = jnp.where(has_right, lane_place(z_after[0], z_after[1]), 0.0)
    big = jnp.concatenate([center, jnp.zeros((8, 128), F32)], axis=0)
    big = pltpu.roll(big, 7, 0)
    r_b = lax.broadcasted_iota(jnp.int32, (16, 128), 0)
    before = jnp.where(r_b >= 1, before, 0.0)
    before = jnp.concatenate([before, jnp.zeros((span - 16, 128), F32)], axis=0)
    before = pltpu.roll(before, span - 1, 0)
    after = jnp.concatenate([after, jnp.zeros((span - 8, 128), F32)], axis=0)
    after = pltpu.roll(after, frames + 7, 0)
    pos = lax.broadcasted_iota(jnp.int32, (span, 128), 0) - 8 + tm * frames
    whole = jnp.where((pos >= 0) & (pos < n_tm * frames), big + before + after, 0.0)
    turned[...] = jnp.transpose(
        jnp.concatenate([whole[8 : 8 + frames], jnp.zeros((128 - frames, 128), F32)], axis=0)
    )
    mel_out[...] = turned[pl.ds(pl.multiple_of(f * bins, 8), bins), 0:frames]

    m = whole.astype(BF16).astype(F32)
    n_taps, mels = pre.shape[0], pre.shape[-1]
    width = feats.shape[2]
    for k in range(n_taps):
        s = (n_taps // 2 - k) % span
        taps_in[:, k * mels : (k + 1) * mels] = (pltpu.roll(m, s, 0) if s else m).astype(BF16)
    if fused:
        gather_end()
    else:
        own_pre.wait()
    made = jnp.zeros((span, width), F32)
    for k in range(n_taps):
        made = made + dot_nt(taps_in[:, k * mels : (k + 1) * mels], pre[k].reshape(width, mels))
    pos = lax.broadcasted_iota(jnp.int32, (span, width), 0) - 8 + tm * frames
    made = made + jnp.concatenate(
        [pre_bias[pl.ds(f * (width // 128) + i, 1), :] for i in range(width // 128)], axis=1
    )
    feats[f] = jnp.where((pos >= 0) & (pos < n_tm * frames), made, 0.0).astype(BF16)
    swap = remote(feats.at[f], feats.at[f], ft_send, ft_recv, partner)
    swap.start()
    load_up.wait()

    group = wide_f.shape[1] // k_taps
    rep = 128 * k_taps

    def upsample(h):
        x = feats[h].astype(F32)
        mid = x[8 : 8 + frames].astype(BF16)
        prev = pltpu.roll(x, 1, 0)[8 : 8 + frames].astype(BF16)
        later = pltpu.roll(x, span - 1, 0)[8 : 8 + frames].astype(BF16)
        for g in range(width // group):
            for t in range(group // 128):
                cols = slice(g * group + t * 128, g * group + t * 128 + 128)
                for half_of, pair in enumerate(((mid, prev), (later, mid))):
                    both = jnp.concatenate([v[:, cols] for v in pair], axis=1)
                    wide = dot(both, repeat[half_of]).astype(BF16)
                    for p in range(2):
                        top = (2 * half_of + p) * frames
                        wide_f[top : top + frames, t * rep : (t + 1) * rep] = wide[:, p * rep : (p + 1) * rep]
            row = pl.multiple_of((h * width + g * group) * k_taps, 128)
            acc[...] += dot(wide_f[...], up[pl.ds(row, group * k_taps), :])

    upsample(f)
    swap.wait()
    upsample(other)
    bias = jnp.concatenate([up_bias[i : i + 1, :] for i in range(up_bias.shape[0])], axis=1)
    done = acc[...] + bias
    r = lax.broadcasted_iota(jnp.int32, (4 * frames, 4 * frames), 0)
    c = lax.broadcasted_iota(jnp.int32, (4 * frames, 4 * frames), 1)
    perm = (r == lax.rem(c, 4) * frames + c // 4).astype(F32).astype(BF16)
    vocal[...] = dot(jnp.transpose(done).astype(BF16), perm).astype(BF16)


def shards(
    latent, mel_noisy, time_shift, first_gain, first_shift, conv_first, second_gain,
    second_shift, conv_second, second_bias, out_proj, pre_weight, pre_bias, up_weight, up_bias,
):
    chans, bins, frames = latent.shape
    n_tm, n_f = lax.axis_size("tm"), lax.axis_size("freq")
    n = n_tm * n_f
    lat = jnp.transpose(latent, (1, 2, 0))
    vec = lambda v: v.reshape(1, -1)
    vmem = pl.BlockSpec(memory_space=pltpu.VMEM)
    hbm = pl.BlockSpec(memory_space=pl.ANY)
    span = frames + 16
    dma = pltpu.SemaphoreType.DMA
    pre = jnp.transpose(pre_weight, (1, 0, 2))
    n_taps, rows, mels = pre.shape
    k_taps, outs = up_weight.shape[1], up_weight.shape[2]
    half = n_tm * rows // n_f
    fused = rows % 32 == 0 and n_tm % 4 == 0 and lax.axis_size("song") == 2
    if fused:
        held = (n_taps, n_tm // n_f, rows, mels)
    else:
        held = (n_taps, half, mels)
        pre = lax.all_gather(pre, "tm", axis=1, tiled=True)
        pre = lax.dynamic_slice_in_dim(pre, lax.axis_index("freq") * half, half, axis=1)
    operands = (
        lat, mel_noisy, vec(time_shift), vec(first_gain), vec(first_shift),
        conv_first.reshape(9 * chans, chans), vec(second_gain), vec(second_shift),
        conv_second.reshape(9, chans, chans), vec(second_bias), vec(out_proj),
        pre, pre_bias.reshape(-1, 128), up_weight.reshape(-1, outs),
        up_bias.reshape(-1, 128),
    )
    copies = [pltpu.VMEM(x.shape, x.dtype) for x in operands[:11] + (operands[12], operands[14])]
    return pl.pallas_call(
        functools.partial(block_kernel, n_tm, n_f, fused),
        out_shape=(
            jax.ShapeDtypeStruct((bins, frames), F32),
            jax.ShapeDtypeStruct((outs, 4 * frames), BF16),
        ),
        in_specs=[hbm] * 15,
        out_specs=(vmem, vmem),
        scratch_shapes=copies + [
            pltpu.VMEM(held, BF16),
            pltpu.VMEM(operands[13].shape, BF16),
            pltpu.VMEM((n, 1, 2 * chans), F32),
            pltpu.VMEM((n, 1, 2 * chans), F32),
            pltpu.VMEM((bins, chans), BF16),
            pltpu.VMEM((bins, chans), BF16),
            pltpu.VMEM((bins, chans), BF16),
            pltpu.VMEM((bins, chans), BF16),
            pltpu.VMEM((frames, chans), BF16),
            pltpu.VMEM((16, chans), BF16),
            pltpu.VMEM((16, chans), BF16),
            pltpu.VMEM((bins, chans), F32),
            pltpu.VMEM((bins, chans), F32),
            pltpu.VMEM((bins + 2, frames, 3 * chans), BF16),
            pltpu.VMEM((bins, frames, chans), BF16),
            pltpu.VMEM((3, bins + 16, 8, 128), F32),
            pltpu.VMEM((frames + 8, 128), F32),
            pltpu.VMEM((frames + 8, 128), F32),
            pltpu.VMEM((2, 16, 128), F32),
            pltpu.VMEM((2, 8, 128), F32),
            pltpu.VMEM((128, 128), F32),
            pltpu.VMEM((span, n_taps * mels), BF16),
            pltpu.VMEM((2, 256, 256 * k_taps), BF16),
            pltpu.VMEM((2, span, half), BF16),
            pltpu.VMEM((4 * frames, 384 * k_taps), BF16),
            pltpu.VMEM((4 * frames, outs), F32),
            dma((13,)), dma, dma,
            dma((n,)), dma((n,)), dma((n,)), dma((n,)),
            dma((5,)), dma((5,)), dma((5,)), dma((5,)),
            dma((n_tm // 2, 2)), dma((n_tm // 2, 2)), dma((n_tm // 2, 3)), dma, dma,
        ],
        compiler_params=pltpu.CompilerParams(
            collective_id=0, has_side_effects=True, vmem_limit_bytes=56 * 2**20
        ),
        cost_estimate=pl.CostEstimate(
            flops=2 * 9 * bins * frames * chans * chans, bytes_accessed=15 * 2**20, transcendentals=0
        ),
    )(*operands)


def solution(mesh):
    in_specs = (
        P(None, "freq", ("song", "tm")),
        P("freq", ("song", "tm")),
        P("song"),
        P(),
        P(),
        P(),
        P(),
        P(),
        P(),
        P(),
        P(),
        P("tm", None, None),
        P(),
        P(None, None, "freq"),
        P("freq"),
    )
    out_specs = (P("freq", ("song", "tm")), P("freq", ("song", "tm")))
    return jax.shard_map(shards, mesh=mesh, in_specs=in_specs, out_specs=out_specs, check_vma=False)
```

```python
import functools

import jax
import jax.numpy as jnp
from jax import lax
from jax.experimental import pallas as pl
from jax.experimental.pallas import tpu as pltpu
from jax.sharding import PartitionSpec as P

GROUPS = 32
EPSILON = 1e-05
STEP_SIZE = 0.25
MESH = pl.DeviceIdType.MESH
F32 = jnp.float32
BF16 = jnp.bfloat16
NT = (((1,), (1,)), ((), ()))


def dot(a, b):
    return jnp.dot(a, b, preferred_element_type=F32)


def dot_nt(a, b):
    return lax.dot_general(a, b, NT, preferred_element_type=F32)


def three_parts(x):
    hi = x.astype(BF16)
    rest = x - hi.astype(F32)
    mid = rest.astype(BF16)
    low = (rest - mid.astype(F32)).astype(BF16)
    return hi, mid, low


def block_kernel(
    n_tm, n_f, fused,
    lat_h, mel_h, tshift_h, gain1_h, shift1_h, w1_h, gain2_h, shift2_h, w2_h, bias2_h, proj_h,
    pre_h, pre_bias_h, up_h, up_bias_h,
    mel_out, vocal,
    lat, mel, tshift, gain1, shift1, w1, gain2, shift2, w2, bias2, proj, pre_bias, up_bias,
    pre, up,
    stats1, stats2, stage_l, stage_r, halo_l, halo_r, halo_b, corner_l, corner_r,
    act_l, act_r, spread, first, gpad, zt, z_part, z_before, z_after, turned,
    taps_in, repeat, feats, wide_f, acc,
    in_sem, up_sem, own_sem,
    s1_send, s1_recv, s2_send, s2_recv, h_send, h_recv, z_send, z_recv,
    p_send, p_recv, fw_send, ft_send, ft_recv,
):
    bins, frames, chans = lat.shape
    n = n_tm * n_f
    tm = lax.axis_index("tm")
    f = lax.axis_index("freq")
    me = tm * n_f + f
    other = 1 - f
    has_left = tm > 0
    has_right = tm < n_tm - 1

    def peer_of(k):
        p = lax.rem(me + k, n)
        return p, {"tm": p // n_f, "freq": lax.rem(p, n_f)}

    barrier = pltpu.get_barrier_semaphore()
    loads = [
        pltpu.make_async_copy(src, dst, in_sem.at[i])
        for i, (src, dst) in enumerate([
            (lat_h, lat), (w2_h, w2), (w1_h, w1), (mel_h, mel), (tshift_h, tshift), (gain1_h, gain1),
            (shift1_h, shift1), (gain2_h, gain2), (shift2_h, shift2), (bias2_h, bias2), (proj_h, proj),
            (pre_bias_h, pre_bias), (up_bias_h, up_bias),
        ])
    ]

    def greet(k, c):
        pl.semaphore_signal(barrier, inc=1, device_id=peer_of(k)[1], device_id_type=MESH)
        return c

    lax.fori_loop(1, n, greet, 0, unroll=n <= 16)
    song = lax.axis_index("song")
    beside = tm + 1 - 2 * lax.rem(tm, 2)
    across = [{"song": 1 - song, "tm": tm, "freq": f}, {"song": 1 - song, "tm": beside, "freq": f}]
    if fused:
        for to in across:
            pl.semaphore_signal(barrier, inc=1, device_id=to, device_id_type=MESH)
    for c in loads:
        c.start()
    acc[...] = jnp.zeros(acc.shape, F32)
    gpad[...] = jnp.zeros(gpad.shape, F32)

    k_taps = repeat.shape[2] // 256
    r = lax.broadcasted_iota(jnp.int32, repeat.shape[1:], 0)
    c = lax.broadcasted_iota(jnp.int32, (1, repeat.shape[2]), 1)
    tap = lax.rem(c, k_taps)
    chan = lax.rem(c // k_taps, 128)
    source = jnp.where(tap >= 4, chan + 128, chan)
    turn = lax.rem(tap, 4) - c // (128 * k_taps)
    for g in range(2):
        wanted = jnp.where(turn == 2 - 2 * g, source, -1)
        repeat[g] = jnp.where(r == wanted, 1.0, 0.0).astype(BF16)
    loads[0].wait()
    load_up = pltpu.make_async_copy(up_h, up, up_sem)
    load_up.start()

    sub8 = lax.broadcasted_iota(jnp.int32, (bins, 8, chans), 1)
    head = lat[:, 0:16, :].astype(F32)[:, 0:8, :]
    tail = lat[:, frames - 16 : frames, :].astype(F32)[:, 8:16, :]
    stage_l[...] = jnp.sum(jnp.where(sub8 == 0, head, 0.0), axis=1).astype(BF16)
    stage_r[...] = jnp.sum(jnp.where(sub8 == 7, tail, 0.0), axis=1).astype(BF16)

    def remote(src, dst, send, recv, to):
        return pltpu.make_async_remote_copy(
            src_ref=src, dst_ref=dst, send_sem=send, recv_sem=recv, device_id=to, device_id_type=MESH
        )

    edge = pl.multiple_of((1 - f) * (bins - 16), 16)
    to_left = [{"tm": tm - 1, "freq": f}, {"tm": tm - 1, "freq": other}]
    to_right = [{"tm": tm + 1, "freq": f}, {"tm": tm + 1, "freq": other}]
    partner = {"tm": tm, "freq": other}
    h_bin = remote(lat.at[(1 - f) * (bins - 1)], halo_b, h_send.at[0], h_recv.at[0], partner)
    go_left = [
        remote(stage_l, halo_r, h_send.at[1], h_recv.at[1], to_left[0]),
        remote(stage_l.at[pl.ds(edge, 16)], corner_r, h_send.at[2], h_recv.at[2], to_left[1]),
    ]
    go_right = [
        remote(stage_r, halo_l, h_send.at[3], h_recv.at[3], to_right[0]),
        remote(stage_r.at[pl.ds(edge, 16)], corner_l, h_send.at[4], h_recv.at[4], to_right[1]),
    ]

    def fold(x):
        return jnp.sum(x.reshape(-1, 8, chans), axis=0)

    def stat_step(b, carry):
        s, q = carry
        x = lat[pl.ds(b * 4, 4)].astype(F32)
        return s + fold(x), q + fold(x * x)

    zero8 = jnp.zeros((8, chans), F32)
    s, q = lax.fori_loop(0, bins // 4, stat_step, (zero8, zero8))

    def send_stats(s, q, stats, send, recv):
        stats[me] = jnp.concatenate(
            [jnp.sum(s, axis=0, keepdims=True), jnp.sum(q, axis=0, keepdims=True)], axis=1
        )

        def go(k, c):
            _, to = peer_of(k)
            remote(stats.at[me], stats.at[me], send.at[k], recv.at[me], to).start()
            return c

        lax.fori_loop(1, n, go, 0, unroll=n <= 16)

    def take_stats(stats, send, recv):
        def wait(k, c):
            p, to = peer_of(k)
            remote(stats.at[me], stats.at[p], send.at[k], recv.at[p], to).wait_recv()
            return c

        lax.fori_loop(1, n, wait, 0, unroll=n <= 16)
        total = jnp.sum(stats[...], axis=0)
        both = jnp.concatenate(
            [
                jnp.broadcast_to(total[:, :chans], (8, chans)),
                jnp.broadcast_to(total[:, chans:], (8, chans)),
            ],
            axis=0,
        )
        size = chans // GROUPS
        gi = lax.broadcasted_iota(jnp.int32, (chans, chans), 0) // size
        gj = lax.broadcasted_iota(jnp.int32, (chans, chans), 1) // size
        same = (gi == gj).astype(F32)
        sums = jnp.dot(both, same, preferred_element_type=F32, precision=lax.Precision.HIGHEST)
        count = float(size * bins * frames * n)
        mean = sums[0:1] / count
        var = sums[8:9] / count - mean * mean
        return mean, lax.rsqrt(var + EPSILON)

    def end_stats(stats, send, recv):
        def wait(k, c):
            p, to = peer_of(k)
            remote(stats.at[me], stats.at[me], send.at[k], recv.at[me], to).wait_send()
            return c

        lax.fori_loop(1, n, wait, 0, unroll=n <= 16)

    pl.semaphore_wait(barrier, n + 1 if fused else n - 1)
    send_stats(s, q, stats1, s1_send, s1_recv)
    h_bin.start()

    @pl.when(has_left)
    def _():
        for c in go_left:
            c.start()

    @pl.when(has_right)
    def _():
        for c in go_right:
            c.start()

    half_n = n_tm // n_f
    slot = lax.rem(tm, half_n)
    holder = f == tm // half_n
    parity = lax.rem(tm, 2)
    part_rows = pre.shape[-2] // 2

    def piece_of(d, h):
        return pre.at[:, d, pl.ds(pl.multiple_of(h * part_rows, 16), part_rows)]

    def push(k, h):
        to = jnp.where(k == 0, beside, lax.rem(tm + 2 * k, n_tm))
        src = pre_h.at[:, pl.ds(pl.multiple_of(h * part_rows, 16), part_rows)]
        return remote(src, piece_of(slot, h), p_send.at[k, h], p_recv.at[slot, h], {"tm": to, "freq": f})

    def forwards(d):
        return [
            remote(piece_of(d, song), piece_of(d, song), fw_send.at[d, i], p_recv.at[d, song], to)
            for i, to in enumerate([{"tm": beside, "freq": f}] + across)
        ]

    def arrived(d, h):
        remote(piece_of(d, h), piece_of(d, h), fw_send.at[d, 0], p_recv.at[d, h], across[0]).wait_recv()

    if fused:
        own_pre = pltpu.make_async_copy(pre_h, pre.at[:, slot], own_sem)
    else:
        own_pre = pltpu.make_async_copy(pre_h, pre, own_sem)
        own_pre.start()

    def gather_start():
        @pl.when(holder)
        def _():
            own_pre.start()

            def go(k, c):
                push(k, song).start()
                return c

            lax.fori_loop(0, n_tm // 2, go, 0)
            push(0, 1 - song).start()

    def gather_forward():
        def go(j, c):
            d = 2 * j + parity

            @pl.when(d + f * half_n != tm)
            def _():
                arrived(d, song)
                for copy in forwards(d):
                    copy.start()

            return c

        lax.fori_loop(0, half_n // 2, go, 0)

    def gather_end():
        @pl.when(holder)
        def _():
            own_pre.wait()

            def wait(k, c):
                push(k, song).wait_send()
                return c

            lax.fori_loop(0, n_tm // 2, wait, 0)
            push(0, 1 - song).wait_send()

        def rest(j, c):
            d = 2 * j + parity

            @pl.when(d + f * half_n != tm)
            def _():
                arrived(d, 1 - song)
                for copy in forwards(d):
                    copy.wait_send()

            e = 2 * j + 1 - parity
            arrived(e, 0)
            arrived(e, 1)
            return c

        lax.fori_loop(0, half_n // 2, rest, 0)

    if fused:
        gather_start()

    for c in loads[1:]:
        c.wait()


    p_row = proj[...]
    hi, mid, low = [x.astype(F32) for x in three_parts(p_row)]
    row = lax.broadcasted_iota(jnp.int32, (16, chans), 0)
    parts = jnp.where(row == 0, hi, jnp.where(row == 1, mid, jnp.where(row == 2, low, 0.0))).astype(BF16)
    row24 = lax.broadcasted_iota(jnp.int32, (32, chans), 0)
    taps = jnp.zeros((32, chans), F32)
    for i in range(3):
        for j in range(3):
            wv = jnp.sum(dot_nt(parts, w2[3 * i + j]), axis=0, keepdims=True)
            a, b, _ = three_parts(wv)
            taps = jnp.where(row24 == 8 * j + i, a.astype(F32), taps)
            taps = jnp.where(row24 == 8 * j + 3 + i, b.astype(F32), taps)
    taps = taps.astype(BF16)
    direct = jnp.where(row24 == 9, hi, jnp.where(row24 == 12, mid, jnp.where(row24 == 14, low, 0.0))).astype(BF16)
    const = jnp.sum(p_row * bias2[...], axis=1, keepdims=True)

    h_bin.wait()

    @pl.when(has_left)
    def _():
        for c in go_left:
            c.wait_send()
        for c in go_right:
            c.wait_recv()

    @pl.when(has_right)
    def _():
        for c in go_right:
            c.wait_send()
        for c in go_left:
            c.wait_recv()

    mean, inv = take_stats(stats1, s1_send, s1_recv)
    scale = inv * gain1[...]
    shift = shift1[...]

    def silu(x, mean, scale, shift):
        y = (x - mean) * scale + shift
        h = 0.5 * y
        return h + h * jnp.tanh(h)

    left_on = jnp.where(has_left, 1.0, 0.0).astype(F32)
    right_on = jnp.where(has_right, 1.0, 0.0).astype(F32)

    def edge_act(ref, present):
        x = ref[...].astype(F32)
        return jnp.where(present, silu(x, mean, scale, shift), 0.0)

    act_l[...] = edge_act(halo_l, has_left)
    act_r[...] = edge_act(halo_r, has_right)
    cl = edge_act(corner_l, has_left)
    cr = edge_act(corner_r, has_right)
    pick = f * 15
    r16 = lax.broadcasted_iota(jnp.int32, (16, chans), 0)
    cl = jnp.sum(jnp.where(r16 == pick, cl, 0.0), axis=0, keepdims=True)
    cr = jnp.sum(jnp.where(r16 == pick, cr, 0.0), axis=0, keepdims=True)
    rows = lax.broadcasted_iota(jnp.int32, (frames, chans), 0)

    def put(at, x, left, right):
        spread[at, :, 0:chans] = jnp.where(rows == 0, left, pltpu.roll(x, 1, 0)).astype(BF16)
        spread[at, :, chans : 2 * chans] = x.astype(BF16)
        spread[at, :, 2 * chans : 3 * chans] = jnp.where(
            rows == frames - 1, right, pltpu.roll(x, frames - 1, 0)
        ).astype(BF16)

    put((1 - f) * (bins + 1), silu(halo_b[...].astype(F32), mean, scale, shift), cl, cr)
    spread[f * (bins + 1)] = jnp.zeros(spread.shape[1:], BF16)

    nb = 8
    moved = tshift[...]

    def norm_bins(start, end):
        for at in range(start, min(end, bins)):
            x = silu(lat[at].astype(F32), mean, scale, shift)
            put(at + 1, x, act_l[at : at + 1, :], act_r[at : at + 1, :])

    s, q = zero8, zero8
    norm_bins(0, nb + 1)
    for b in range(0, bins, nb):
        part = jnp.concatenate(
            [spread[b + i : b + i + nb].reshape(nb * frames, 3 * chans) for i in range(3)], axis=1
        )
        out = (dot(part, w1[...]) + moved).astype(BF16)
        norm_bins(b + nb + 1, b + 2 * nb + 1)
        first[b : b + nb] = out.reshape(nb, frames, chans)
        x = out.astype(F32)
        s, q = s + fold(x), q + fold(x * x)
    send_stats(s, q, stats2, s2_send, s2_recv)
    end_stats(stats1, s1_send, s1_recv)

    if fused:
        gather_forward()
    vb = 4
    sub = lax.broadcasted_iota(jnp.int32, (8, frames), 0)

    def direct_step(b, c):
        raw = lat[pl.ds(b * vb, vb)].reshape(vb * frames, chans)
        g = dot_nt(direct, raw)
        for u in range(vb):
            at = b * vb + u
            own = mel[pl.ds(at, 1), :] * (1.0 / STEP_SIZE) + const
            piece = g[8:16, u * frames : (u + 1) * frames]
            gpad[1, at + 2, :, 0:frames] = jnp.where(sub == 7, own, piece)
        return c

    lax.fori_loop(0, bins // vb, direct_step, 0)

    mean2, inv2 = take_stats(stats2, s2_send, s2_recv)
    scale2 = inv2 * gain2[...]
    low2 = shift2[...]

    def tap_step(b, c):
        x = first[pl.ds(b * vb, vb)].reshape(vb * frames, chans).astype(F32)
        act = silu(x, mean2, scale2, low2).astype(BF16)
        g = dot_nt(taps, act)
        for u in range(vb):
            at = b * vb + u
            for j in range(3):
                piece = g[8 * j : 8 * j + 8, u * frames : (u + 1) * frames]
                if j == 1:
                    piece = piece + gpad[j, at + 2, :, 0:frames]
                gpad[j, at + 2, :, 0:frames] = piece
        return c

    lax.fori_loop(0, bins // vb, tap_step, 0, unroll=4)
    end_stats(stats2, s2_send, s2_recv)

    tall = bins + 8
    subs = lax.broadcasted_iota(jnp.int32, (tall, 8, 128), 1)
    total = jnp.zeros((tall, 128), F32)
    for j in range(3):
        comb = jnp.zeros((tall, 8, 128), F32)
        for i in range(3):
            mine = (subs == i) | (subs == i + 3)
            if i == 1:
                mine = mine | (subs >= 6)
            comb = jnp.where(mine, gpad[j, i : i + tall], comb)
        rowsum = jnp.sum(comb, axis=1)
        total = total + (pltpu.roll(rowsum, 2 - j, 1) if j < 2 else rowsum)
    z = jnp.concatenate([total * STEP_SIZE, jnp.zeros((128 - tall, 128), F32)], axis=0)
    wide = frames + 8
    zt[...] = jnp.transpose(z)[0:wide]

    top = frames - 8
    z_own = remote(zt, z_part, z_send.at[0], z_recv.at[0], partner)
    z_left = [
        remote(zt.at[pl.ds(0, 8)], z_after.at[0], z_send.at[1], z_recv.at[1], to_left[0]),
        remote(zt.at[pl.ds(0, 8)], z_after.at[1], z_send.at[2], z_recv.at[2], to_left[1]),
    ]
    z_right = [
        remote(zt.at[pl.ds(top, 16)], z_before.at[0], z_send.at[3], z_recv.at[3], to_right[0]),
        remote(zt.at[pl.ds(top, 16)], z_before.at[1], z_send.at[4], z_recv.at[4], to_right[1]),
    ]

    @pl.when(has_left)
    def _():
        for c in z_left:
            c.start()

    @pl.when(has_right)
    def _():
        for c in z_right:
            c.start()

    z_own.start()

    @pl.when(has_left)
    def _():
        for c in z_left:
            c.wait_send()
        for c in z_right:
            c.wait_recv()

    @pl.when(has_right)
    def _():
        for c in z_right:
            c.wait_send()
        for c in z_left:
            c.wait_recv()

    z_own.wait()

    def lane_place(mine, theirs):
        shape = mine.shape
        lane = lax.broadcasted_iota(jnp.int32, shape, 1)
        low = jnp.where(f == 0, mine, theirs)
        high = jnp.where(f == 0, theirs, mine)
        low = jnp.where(lane <= bins, pltpu.roll(low, 127, 1), 0.0)
        high = jnp.where(lane >= bins - 1, pltpu.roll(high, bins - 1, 1), 0.0)
        return low + high

    span = frames + 16
    center = lane_place(zt[...], z_part[...])
    before = jnp.where(has_left, lane_place(z_before[0], z_before[1]), 0.0)
    after = jnp.where(has_right, lane_place(z_after[0], z_after[1]), 0.0)
    big = jnp.concatenate([center, jnp.zeros((8, 128), F32)], axis=0)
    big = pltpu.roll(big, 7, 0)
    r_b = lax.broadcasted_iota(jnp.int32, (16, 128), 0)
    before = jnp.where(r_b >= 1, before, 0.0)
    before = jnp.concatenate([before, jnp.zeros((span - 16, 128), F32)], axis=0)
    before = pltpu.roll(before, span - 1, 0)
    after = jnp.concatenate([after, jnp.zeros((span - 8, 128), F32)], axis=0)
    after = pltpu.roll(after, frames + 7, 0)
    pos = lax.broadcasted_iota(jnp.int32, (span, 128), 0) - 8 + tm * frames
    whole = jnp.where((pos >= 0) & (pos < n_tm * frames), big + before + after, 0.0)
    turned[...] = jnp.transpose(
        jnp.concatenate([whole[8 : 8 + frames], jnp.zeros((128 - frames, 128), F32)], axis=0)
    )
    mel_out[...] = turned[pl.ds(pl.multiple_of(f * bins, 8), bins), 0:frames]

    m = whole.astype(BF16).astype(F32)
    n_taps, mels = pre.shape[0], pre.shape[-1]
    width = feats.shape[2]
    for k in range(n_taps):
        s = (n_taps // 2 - k) % span
        taps_in[:, k * mels : (k + 1) * mels] = (pltpu.roll(m, s, 0) if s else m).astype(BF16)
    if fused:
        gather_end()
    else:
        own_pre.wait()
    made = jnp.zeros((span, width), F32)
    for k in range(n_taps):
        made = made + dot_nt(taps_in[:, k * mels : (k + 1) * mels], pre[k].reshape(width, mels))
    pos = lax.broadcasted_iota(jnp.int32, (span, width), 0) - 8 + tm * frames
    made = made + jnp.concatenate(
        [pre_bias[pl.ds(f * (width // 128) + i, 1), :] for i in range(width // 128)], axis=1
    )
    feats[f] = jnp.where((pos >= 0) & (pos < n_tm * frames), made, 0.0).astype(BF16)
    swap = remote(feats.at[f], feats.at[f], ft_send, ft_recv, partner)
    swap.start()
    load_up.wait()

    group = wide_f.shape[1] // k_taps
    rep = 128 * k_taps

    def upsample(h):
        x = feats[h].astype(F32)
        mid = x[8 : 8 + frames].astype(BF16)
        prev = pltpu.roll(x, 1, 0)[8 : 8 + frames].astype(BF16)
        later = pltpu.roll(x, span - 1, 0)[8 : 8 + frames].astype(BF16)
        for g in range(width // group):
            for t in range(group // 128):
                cols = slice(g * group + t * 128, g * group + t * 128 + 128)
                for half_of, pair in enumerate(((mid, prev), (later, mid))):
                    both = jnp.concatenate([v[:, cols] for v in pair], axis=1)
                    wide = dot(both, repeat[half_of]).astype(BF16)
                    for p in range(2):
                        top = (2 * half_of + p) * frames
                        wide_f[top : top + frames, t * rep : (t + 1) * rep] = wide[:, p * rep : (p + 1) * rep]
            row = pl.multiple_of((h * width + g * group) * k_taps, 128)
            acc[...] += dot(wide_f[...], up[pl.ds(row, group * k_taps), :])

    upsample(f)
    swap.wait()
    upsample(other)
    bias = jnp.concatenate([up_bias[i : i + 1, :] for i in range(up_bias.shape[0])], axis=1)
    done = acc[...] + bias
    r = lax.broadcasted_iota(jnp.int32, (4 * frames, 4 * frames), 0)
    c = lax.broadcasted_iota(jnp.int32, (4 * frames, 4 * frames), 1)
    perm = (r == lax.rem(c, 4) * frames + c // 4).astype(F32).astype(BF16)
    vocal[...] = dot(jnp.transpose(done).astype(BF16), perm).astype(BF16)


def shards(
    latent, mel_noisy, time_shift, first_gain, first_shift, conv_first, second_gain,
    second_shift, conv_second, second_bias, out_proj, pre_weight, pre_bias, up_weight, up_bias,
):
    chans, bins, frames = latent.shape
    n_tm, n_f = lax.axis_size("tm"), lax.axis_size("freq")
    n = n_tm * n_f
    lat = jnp.transpose(latent, (1, 2, 0))
    vec = lambda v: v.reshape(1, -1)
    vmem = pl.BlockSpec(memory_space=pltpu.VMEM)
    hbm = pl.BlockSpec(memory_space=pl.ANY)
    span = frames + 16
    dma = pltpu.SemaphoreType.DMA
    pre = jnp.transpose(pre_weight, (1, 0, 2))
    n_taps, rows, mels = pre.shape
    k_taps, outs = up_weight.shape[1], up_weight.shape[2]
    half = n_tm * rows // n_f
    fused = rows % 32 == 0 and n_tm % 4 == 0 and lax.axis_size("song") == 2
    if fused:
        held = (n_taps, n_tm // n_f, rows, mels)
    else:
        held = (n_taps, half, mels)
        pre = lax.all_gather(pre, "tm", axis=1, tiled=True)
        pre = lax.dynamic_slice_in_dim(pre, lax.axis_index("freq") * half, half, axis=1)
    operands = (
        lat, mel_noisy, vec(time_shift), vec(first_gain), vec(first_shift),
        conv_first.reshape(9 * chans, chans), vec(second_gain), vec(second_shift),
        conv_second.reshape(9, chans, chans), vec(second_bias), vec(out_proj),
        pre, pre_bias.reshape(-1, 128), up_weight.reshape(-1, outs),
        up_bias.reshape(-1, 128),
    )
    copies = [pltpu.VMEM(x.shape, x.dtype) for x in operands[:11] + (operands[12], operands[14])]
    return pl.pallas_call(
        functools.partial(block_kernel, n_tm, n_f, fused),
        out_shape=(
            jax.ShapeDtypeStruct((bins, frames), F32),
            jax.ShapeDtypeStruct((outs, 4 * frames), BF16),
        ),
        in_specs=[hbm] * 15,
        out_specs=(vmem, vmem),
        scratch_shapes=copies + [
            pltpu.VMEM(held, BF16),
            pltpu.VMEM(operands[13].shape, BF16),
            pltpu.VMEM((n, 1, 2 * chans), F32),
            pltpu.VMEM((n, 1, 2 * chans), F32),
            pltpu.VMEM((bins, chans), BF16),
            pltpu.VMEM((bins, chans), BF16),
            pltpu.VMEM((bins, chans), BF16),
            pltpu.VMEM((bins, chans), BF16),
            pltpu.VMEM((frames, chans), BF16),
            pltpu.VMEM((16, chans), BF16),
            pltpu.VMEM((16, chans), BF16),
            pltpu.VMEM((bins, chans), F32),
            pltpu.VMEM((bins, chans), F32),
            pltpu.VMEM((bins + 2, frames, 3 * chans), BF16),
            pltpu.VMEM((bins, frames, chans), BF16),
            pltpu.VMEM((3, bins + 16, 8, 128), F32),
            pltpu.VMEM((frames + 8, 128), F32),
            pltpu.VMEM((frames + 8, 128), F32),
            pltpu.VMEM((2, 16, 128), F32),
            pltpu.VMEM((2, 8, 128), F32),
            pltpu.VMEM((128, 128), F32),
            pltpu.VMEM((span, n_taps * mels), BF16),
            pltpu.VMEM((2, 256, 256 * k_taps), BF16),
            pltpu.VMEM((2, span, half), BF16),
            pltpu.VMEM((4 * frames, 384 * k_taps), BF16),
            pltpu.VMEM((4 * frames, outs), F32),
            dma((13,)), dma, dma,
            dma((n,)), dma((n,)), dma((n,)), dma((n,)),
            dma((5,)), dma((5,)), dma((5,)), dma((5,)),
            dma((n_tm // 2, 2)), dma((n_tm // 2, 2)), dma((n_tm // 2, 3)), dma, dma,
        ],
        compiler_params=pltpu.CompilerParams(
            collective_id=0, has_side_effects=True, vmem_limit_bytes=56 * 2**20
        ),
        cost_estimate=pl.CostEstimate(
            flops=2 * 9 * bins * frames * chans * chans, bytes_accessed=15 * 2**20, transcendentals=0
        ),
    )(*operands)


def solution(mesh):
    in_specs = (
        P(None, "freq", ("song", "tm")),
        P("freq", ("song", "tm")),
        P("song"),
        P(),
        P(),
        P(),
        P(),
        P(),
        P(),
        P(),
        P(),
        P("tm", None, None),
        P(),
        P(None, None, "freq"),
        P("freq"),
    )
    out_specs = (P("freq", ("song", "tm")), P("freq", ("song", "tm")))
    return jax.shard_map(shards, mesh=mesh, in_specs=in_specs, out_specs=out_specs, check_vma=False)
```
